256 devices in a mesh: group: 8 (over x, y_hi), loop: 32 (over z, y_lo, core).
Axes of the slice: x: 4, y: 4 (y_hi: 2, y_lo: 2; y = y_hi * 2 + y_lo), z: 8, core: 2. Of those that a mesh axis runs over, the one named last changes fastest.
Arguments:
- tile_values: bfloat16 [32, 8, 4, 128, 128], P('loop', 'group'), may hold values from 0 to 20, as said below
- tile_coords: int32 [32, 8, 4], P('loop', 'group'), may hold values from 0 to 15, as said below
- tile_counts: int32 [32, 8], P('loop', 'group'), may hold values from 2 to 4, as said below
- result_coords: int32 [32, 8, 8], P('loop', 'group'), may hold values from 0 to 15, as said below
- result_counts: int32 [32, 8], P('loop', 'group'), may hold values from 4 to 8, as said below
Outputs:
- result_tiles: float32 [32, 8, 8, 128, 128], P('loop', 'group')
The draws below stay inside these ranges and needn't reach their ends.
Inputs may be any that keep to these rules, and one draw needn't show every extreme that they name: `tile_coords`: in each block the first tile_counts slots name distinct positions, and every tile on the matrix's diagonal lying in that block is among them; the other slots name further distinct positions of the block. `tile_counts`: 4 is reached by some block. `result_coords`: in each block the first result_counts slots name distinct positions, and every tile on the matrix's diagonal lying in that block is among them; the other slots name further distinct positions of the block. `result_counts`: 8 is reached by some block. `tile_values`: entries are nonnegative; a diagonal tile's own diagonal entries are 1 or more.
All inputs are finite; a program needn't handle non-finite values.
Results may differ from the reference program's by a relative error of at most 0.0003.
Values may be sent and summed in bfloat16 or wider, within the bound.
No kernel may reach another device: no remote copies, remote signals or barrier semaphores. Data moves between devices by JAX's collectives and lax.ppermute only.
A program may use at most 128 MiB of HBM per device.

```python
import jax
import jax.numpy as jnp
from jax import lax

TILE = 128
BROWS = 2
ROW_BLOCKS = 32
COL_BLOCKS = 8
BCOLS = 8
NROWS = 8192
CAP = 4
CAP_OUT = 8


def pattern_of(key, capacity):
    positions = BROWS * BCOLS
    blocks = ROW_BLOCKS * COL_BLOCKS
    keys = jax.random.split(key, blocks)
    perms = jax.vmap(lambda one_key: jax.random.permutation(one_key, positions))(keys)
    perms = perms.reshape(ROW_BLOCKS, COL_BLOCKS, positions).astype(jnp.int32)
    position_index = jnp.arange(positions, dtype=jnp.int32)
    tile_row = jnp.arange(ROW_BLOCKS, dtype=jnp.int32)[:, None, None] * BROWS + position_index[None, None, :] // BCOLS
    tile_col = jnp.arange(COL_BLOCKS, dtype=jnp.int32)[None, :, None] * BCOLS + position_index[None, None, :] % BCOLS
    scores = perms - jnp.where(tile_row == tile_col, positions, 0).astype(jnp.int32)
    ordered = jnp.argsort(scores, axis=-1).astype(jnp.int32)
    return ordered[..., :capacity]


def counts_of(key, capacity):
    lowest = max(BROWS, capacity // 2)
    drawn = jax.random.randint(key, (ROW_BLOCKS * COL_BLOCKS,), lowest, capacity + 1).astype(jnp.int32)
    chosen = jax.random.randint(jax.random.fold_in(key, 1), (), 0, ROW_BLOCKS * COL_BLOCKS)
    drawn = jnp.where(jnp.arange(ROW_BLOCKS * COL_BLOCKS) == chosen, capacity, drawn).astype(jnp.int32)
    return drawn.reshape(ROW_BLOCKS, COL_BLOCKS)


def draw_tile_values(key, part):
    coords = pattern_of(jax.random.fold_in(key, 11), CAP)
    base_key = jax.random.fold_in(key, 21)
    row_key = jax.random.fold_in(key, 22)
    col_key = jax.random.fold_in(key, 23)
    shape = (ROW_BLOCKS, COL_BLOCKS, CAP, TILE, TILE)
    base = jax.random.uniform(base_key, shape, jnp.float32) ** 2
    along = jnp.arange(NROWS, dtype=jnp.float32) / NROWS
    row_scale = 3.0 ** (0.5 * along) * 10.0 ** (0.5 * jax.random.uniform(row_key, (NROWS,), jnp.float32))
    col_scale = 10.0 ** (0.5 * jax.random.uniform(col_key, (NROWS,), jnp.float32))
    tile_row = jnp.arange(ROW_BLOCKS, dtype=jnp.int32)[:, None, None] * BROWS + coords // BCOLS
    tile_col = jnp.arange(COL_BLOCKS, dtype=jnp.int32)[None, :, None] * BCOLS + coords % BCOLS
    inside = jnp.arange(TILE, dtype=jnp.int32)
    global_rows = tile_row[..., None] * TILE + inside
    global_cols = tile_col[..., None] * TILE + inside
    values = base * row_scale[global_rows][..., :, None] * col_scale[global_cols][..., None, :]
    diagonal = jnp.where(tile_row == tile_col, 1.0, 0.0).astype(jnp.float32)
    values = values + diagonal[..., None, None] * jnp.eye(TILE, dtype=jnp.float32)
    return values.astype(jnp.bfloat16)


def draw_tile_coords(key, part):
    return pattern_of(jax.random.fold_in(key, 11), CAP)


def draw_tile_counts(key, part):
    return counts_of(jax.random.fold_in(key, 12), CAP)


def draw_result_coords(key, part):
    return pattern_of(jax.random.fold_in(key, 13), CAP_OUT)


def draw_result_counts(key, part):
    return counts_of(jax.random.fold_in(key, 14), CAP_OUT)


def setup_inputs(seed: int = 0) -> dict:
    key_of = jax.random.split(jax.random.key(seed), 6)
    tile_values = draw_tile_values(jax.random.fold_in(key_of[5], 71), 0)
    tile_coords = draw_tile_coords(jax.random.fold_in(key_of[5], 71), 0)
    tile_counts = draw_tile_counts(jax.random.fold_in(key_of[5], 71), 0)
    result_coords = draw_result_coords(jax.random.fold_in(key_of[5], 71), 0)
    result_counts = draw_result_counts(jax.random.fold_in(key_of[5], 71), 0)
    return {"tile_values": tile_values, "tile_coords": tile_coords, "tile_counts": tile_counts, "result_coords": result_coords, "result_counts": result_counts}


def dense_blocks(tile_values, tile_coords, tile_counts, positions):
    slot_index = jnp.arange(tile_coords.shape[-1], dtype=jnp.int32)
    in_pattern = slot_index[None, None, :] < tile_counts[:, :, None]
    position_index = jnp.arange(positions, dtype=jnp.int32)
    selector = ((tile_coords[:, :, None, :] == position_index[None, None, :, None]) & in_pattern[:, :, None, :]).astype(jnp.float32)
    return jnp.einsum('abps,absij->abpij', selector, tile_values.astype(jnp.float32), precision=lax.Precision.HIGHEST)


def reference(tile_values, tile_coords, tile_counts, result_coords, result_counts):
    positions = BROWS * BCOLS
    blocks = dense_blocks(tile_values, tile_coords, tile_counts, positions)
    matrix = blocks.reshape(ROW_BLOCKS, COL_BLOCKS, BROWS, BCOLS, TILE, TILE).transpose(0, 2, 4, 1, 3, 5).reshape(NROWS, NROWS)
    product = jnp.dot(matrix, matrix, precision=lax.Precision.HIGHEST, preferred_element_type=jnp.float32)
    product_tiles = product.reshape(ROW_BLOCKS, BROWS, TILE, COL_BLOCKS, BCOLS, TILE).transpose(0, 3, 1, 4, 2, 5).reshape(ROW_BLOCKS, COL_BLOCKS, positions, TILE, TILE)
    chosen = jax.vmap(jax.vmap(lambda tiles_here, where_here: tiles_here[where_here]))(product_tiles, result_coords)
    in_result = jnp.arange(result_coords.shape[-1], dtype=jnp.int32)[None, None, :] < result_counts[:, :, None]
    squared = jnp.where(in_result[..., None, None], chosen * chosen, jnp.float32(0.0))
    column_pick = ((result_coords % BCOLS)[..., None] == jnp.arange(BCOLS, dtype=jnp.int32)).astype(jnp.float32)
    partial_sums = jnp.sum(squared, axis=3)
    totals = jnp.einsum('absc,absj->bcj', column_pick, partial_sums, precision=lax.Precision.HIGHEST)
    column_total = jnp.einsum('absc,bcj->absj', column_pick, totals, precision=lax.Precision.HIGHEST)
    return squared * (NROWS / column_total)[..., None, :]
```

```python
import jax
import jax.numpy as jnp
from jax import lax
from jax.experimental import pallas as pl
from jax.experimental.pallas import tpu as pltpu
from jax.sharding import PartitionSpec as P

TILE = 128
SLOTS = 4
BODY = SLOTS * TILE
UNIT = BODY + 16
WIDE = 9 * TILE
F32, BF16 = jnp.float32, jnp.bfloat16


def loop_perm(f):
    pairs = []
    for i in range(32):
        z, y, c = f(i >> 2, (i >> 1) & 1, i & 1)
        pairs.append((i, (z % 8) * 4 + y * 2 + c))
    return pairs


def group_perm(f):
    pairs = []
    for i in range(8):
        x, y = f(i >> 1, i & 1)
        pairs.append((i, (x % 4) * 2 + y))
    return pairs


CORE = loop_perm(lambda z, y, c: (z, y, 1 - c))
YLO = loop_perm(lambda z, y, c: (z, 1 - y, c))
RING = loop_perm(lambda z, y, c: (z + 1 - 2 * c, y, c))
YHI = group_perm(lambda x, y: (x, 1 - y))
XUP = group_perm(lambda x, y: (x + 1, y))
XDOWN = group_perm(lambda x, y: (x - 1, y))
XFAR = group_perm(lambda x, y: (x + 2, y))


def place(dst, ref, base, row):
    marks = ref[base + BODY : base + UNIT, :].astype(F32)
    for s in range(SLOTS):
        code = jnp.max(marks[s : s + 1, :]).astype(jnp.int32)
        r = (code >= 9).astype(jnp.int32)
        c = code - 9 * r
        rows = pl.ds(pl.multiple_of(row + r * TILE, TILE), TILE)
        cols = pl.ds(pl.multiple_of(c * TILE, TILE), TILE)
        dst[rows, cols] = ref[base + s * TILE : base + (s + 1) * TILE, :]


def where_am_i():
    i = lax.axis_index("loop")
    j = lax.axis_index("group")
    return i >> 2, (i >> 1) & 1, i & 1, j >> 1, j & 1


def expand(coords, counts, *refs):
    right, left = refs[:16], refs[16:20]
    squares, sums, dense_left, dense_right, product = refs[20:]
    z, y, c, x, h = where_am_i()
    dense_left[...] = jnp.zeros_like(dense_left)
    for k, step in enumerate((0, 3, 1, 2)):
        for half in range(2):
            j = ((x + step) & 3) * 2 + (h ^ half)
            place(dense_left.at[j], left[k], half * UNIT, 0)
    product[...] = jnp.zeros_like(product)

    def chunk(first, second, j, y_first, y_second, c_first, c_second):
        dense_right[...] = jnp.zeros_like(dense_right)
        for ref, yy, cc in ((first, y_first, c_first), (second, y_second, c_second)):
            place(dense_right, ref, 0, (yy * 2 + cc) * 256)
            place(dense_right, ref, UNIT, (yy * 2 + 1 - cc) * 256)
        product[...] += jnp.dot(
            dense_left[j, :, : 8 * TILE], dense_right[:, : 8 * TILE], preferred_element_type=F32
        )

    near = y ^ c
    sign = 1 - 2 * c
    chunk(right[0], right[1], z, near, 1 - near, c, c)
    for r in range(1, 4):
        a, b, d, e = right[4 * r - 2 : 4 * r + 2]
        chunk(a, b, (z - sign * r) & 7, near, 1 - near, c, c)
        chunk(d, e, (z + sign * r) & 7, 1 - near, near, 1 - c, 1 - c)
    chunk(right[14], right[15], (z + 4) & 7, near, 1 - near, c, 1 - c)

    column = lax.broadcasted_iota(jnp.int32, (8, TILE), 0)
    total = jnp.zeros((8, TILE), F32)
    for s in range(8):
        p = coords[s]
        rows = pl.ds(pl.multiple_of((p >> 3) * TILE, TILE), TILE)
        cols = pl.ds(pl.multiple_of((p & 7) * TILE, TILE), TILE)
        tile = product[rows, cols]
        tile = jnp.where(s < counts[0], tile * tile, 0.0)
        squares[s] = tile
        part = jnp.sum(tile, axis=0, keepdims=True)
        total += jnp.where(column == (p & 7), part, 0.0)
    for k in range(32):
        sums[k] = total


def rescale(coords, squares, sums, out):
    factor = 8192.0 / jnp.sum(sums[...], axis=0)
    column = lax.broadcasted_iota(jnp.int32, (8, TILE), 0)
    for s in range(8):
        pick = jnp.where(column == (coords[s] & 7), factor, 0.0)
        out[s] = squares[s] * jnp.sum(pick, axis=0, keepdims=True)


def shards(tile_values, tile_coords, tile_counts, result_coords, result_counts):
    slot = jnp.arange(16, dtype=jnp.int32)
    at = jnp.pad(tile_coords[0, 0], (0, 12))
    code = jnp.where(slot < tile_counts[0, 0], at + (at >> 3), 8).astype(BF16)
    unit = jnp.concatenate(
        [tile_values.reshape(BODY, TILE), jnp.broadcast_to(code[:, None], (16, TILE))]
    )
    core = lax.axis_index("loop") & 1

    def along(perm, v):
        return lax.ppermute(v, "loop", perm)

    def across(perm, v):
        return lax.ppermute(v, "group", perm)

    pair = along(CORE, unit)
    beside = along(YLO, unit)
    beside_pair = along(CORE, beside)
    mine = jnp.concatenate([unit, pair])
    theirs = jnp.concatenate([beside, beside_pair])
    first = jnp.where(core == 0, mine, theirs)
    second = jnp.where(core == 0, theirs, mine)
    right = [first, second]
    for r in range(1, 4):
        first, second = along(RING, first), along(RING, second)
        right += [first, second, along(CORE, first), along(CORE, second)]
    first = along(RING, first)
    right += [first, along(CORE, first)]

    row = jnp.concatenate([unit, across(YHI, unit)])
    left = [row, across(XUP, row), across(XDOWN, row), across(XFAR, row)]

    coords, counts = result_coords.reshape(8), result_counts.reshape(1)
    whole = pl.BlockSpec(memory_space=pltpu.VMEM)
    squares, sums = pl.pallas_call(
        expand,
        grid_spec=pltpu.PrefetchScalarGridSpec(
            num_scalar_prefetch=2,
            grid=(),
            in_specs=[whole] * 20,
            out_specs=[whole] * 2,
            scratch_shapes=[
                pltpu.VMEM((8, 256, WIDE), BF16),
                pltpu.VMEM((1024, WIDE), BF16),
                pltpu.VMEM((256, 1024), F32),
            ],
        ),
        out_shape=[
            jax.ShapeDtypeStruct((8, TILE, TILE), F32),
            jax.ShapeDtypeStruct((32, 8, TILE), F32),
        ],
        compiler_params=pltpu.CompilerParams(vmem_limit_bytes=48 * 2**20),
    )(coords, counts, *right, *left)
    sums = lax.all_to_all(sums, "loop", 0, 0, tiled=True)
    out = pl.pallas_call(
        rescale,
        grid_spec=pltpu.PrefetchScalarGridSpec(
            num_scalar_prefetch=1,
            grid=(),
            in_specs=[whole] * 2,
            out_specs=whole,
        ),
        out_shape=jax.ShapeDtypeStruct((8, TILE, TILE), F32),
    )(coords, squares, sums)
    return out[None, None]


def solution(mesh):
    placed = (
        P("loop", "group", None, None, None),
        P("loop", "group", None),
        P("loop", "group"),
        P("loop", "group", None),
        P("loop", "group"),
    )
    return jax.shard_map(
        shards,
        mesh=mesh,
        in_specs=placed,
        out_specs=P("loop", "group", None, None, None),
        check_vma=False,
    )
```

```python
import jax
import jax.numpy as jnp
from jax import lax
from jax.experimental import pallas as pl
from jax.experimental.pallas import tpu as pltpu
from jax.sharding import PartitionSpec as P

TILE = 128
SLOTS = 4
BODY = SLOTS * TILE
UNIT = BODY + 16
WIDE = 9 * TILE
F32, BF16 = jnp.float32, jnp.bfloat16


def loop_perm(f):
    pairs = []
    for i in range(32):
        z, y, c = f(i >> 2, (i >> 1) & 1, i & 1)
        pairs.append((i, (z % 8) * 4 + y * 2 + c))
    return pairs


def group_perm(f):
    pairs = []
    for i in range(8):
        x, y = f(i >> 1, i & 1)
        pairs.append((i, (x % 4) * 2 + y))
    return pairs


CORE = loop_perm(lambda z, y, c: (z, y, 1 - c))
YLO = loop_perm(lambda z, y, c: (z, 1 - y, c))
RING = loop_perm(lambda z, y, c: (z + 1 - 2 * c, y, c))
YHI = group_perm(lambda x, y: (x, 1 - y))
XNEAR = group_perm(lambda x, y: (x ^ 1, y))
XMIRROR = group_perm(lambda x, y: (3 - x, y))


def scalars(ref, base, first, count):
    marks = ref[base + BODY : base + UNIT, :].astype(F32)
    return [jnp.max(marks[s : s + 1, :]).astype(jnp.int32) for s in range(first, first + count)]


def place(dst, ref, base, row):
    for s, code in enumerate(scalars(ref, base, 0, SLOTS)):
        r = (code >= 9).astype(jnp.int32)
        c = code - 9 * r
        rows = pl.ds(pl.multiple_of(row + r * TILE, TILE), TILE)
        cols = pl.ds(pl.multiple_of(c * TILE, TILE), TILE)
        dst[rows, cols] = ref[base + s * TILE : base + (s + 1) * TILE, :]


def where_am_i():
    i = lax.axis_index("loop")
    j = lax.axis_index("group")
    return i >> 2, (i >> 1) & 1, i & 1, j >> 1, j & 1


def multiply(dense_left, dense_right, j, units):
    dense_right[...] = jnp.zeros_like(dense_right)
    for ref, base, y, c in units:
        place(dense_right, ref, base, (y * 2 + c) * 256)
    return jnp.dot(
        dense_left[j, :, : 8 * TILE], dense_right[:, : 8 * TILE], preferred_element_type=F32
    )


def round_units(refs, y, c):
    pair, beside, beside_pair = refs
    return (
        (pair, 0, y, c),
        (pair, UNIT, y, 1 - c),
        (beside, 0, 1 - y, c),
        (beside_pair, 0, 1 - y, 1 - c),
    )


def begin(*refs):
    own, rounds, left = refs[:3], refs[3:15], refs[15:17]
    dense_left, product, dense_right = refs[17:]
    z, y, c, x, h = where_am_i()
    dense_left[...] = jnp.zeros_like(dense_left)
    for k in range(8):
        xx = (x, x ^ 1, 3 - x, (3 - x) ^ 1)[k >> 1]
        place(dense_left.at[xx * 2 + (h ^ (k & 1))], left[k >> 2], (k & 3) * UNIT, 0)
    product[...] = multiply(dense_left, dense_right, z, round_units(own, y, c))
    sign = 1 - 2 * c
    for r in (1, 2):
        near, far = rounds[6 * r - 6 : 6 * r - 3], rounds[6 * r - 3 : 6 * r]
        product[...] += multiply(
            dense_left, dense_right, (z - sign * r) & 7, round_units(near, y, c)
        )
        product[...] += multiply(
            dense_left, dense_right, (z + sign * r) & 7, round_units(far, y, 1 - c)
        )


def proceed(*refs):
    near, far = refs[:3], refs[3:6]
    dense_left, before, product, dense_right = refs[6:]
    z, y, c, _, _ = where_am_i()
    sign = 1 - 2 * c
    product[...] = before[...] + multiply(
        dense_left, dense_right, (z - sign * 3) & 7, round_units(near, y, c)
    )
    product[...] += multiply(
        dense_left, dense_right, (z + sign * 3) & 7, round_units(far, y, 1 - c)
    )


def finish(unit, pair, beside, beside_pair, dense_left, before, squares, sums, dense_right, product, held, sem):
    z, y, c, _, _ = where_am_i()
    units = round_units((pair, beside, beside_pair), y, c)
    product[...] = before[...] + multiply(dense_left, dense_right, (z + 4) & 7, units)
    column = lax.broadcasted_iota(jnp.int32, (8, TILE), 0)
    total = jnp.zeros((8, TILE), F32)
    copies = []
    for s, code in enumerate(scalars(unit, 0, SLOTS, 8)):
        used = code < 16
        p = code & 15
        rows = pl.ds(pl.multiple_of((p >> 3) * TILE, TILE), TILE)
        cols = pl.ds(pl.multiple_of((p & 7) * TILE, TILE), TILE)
        tile = product[rows, cols]
        tile = jnp.where(used, tile * tile, 0.0)
        held[s] = tile
        copies.append(pltpu.make_async_copy(held.at[s], squares.at[s], sem.at[s]))
        copies[-1].start()
        part = jnp.sum(tile, axis=0, keepdims=True)
        total += jnp.where(column == (p & 7), part, 0.0)
    for k in range(32):
        sums[k] = total
    for copy in copies:
        copy.wait()


def rescale(unit, squares, sums, out, marks, inside, parts, done, sem_in, sem_out):
    ins = [pltpu.make_async_copy(sums, parts, sem_in.at[8])]
    ins.append(pltpu.make_async_copy(unit.at[pl.ds(BODY, 16)], marks, sem_in.at[9]))
    ins += [pltpu.make_async_copy(squares.at[s], inside.at[s], sem_in.at[s]) for s in range(8)]
    for copy in ins:
        copy.start()
    ins[1].wait()
    codes = scalars(marks, -BODY, SLOTS, 8)
    ins[0].wait()
    factor = 8192.0 / jnp.sum(parts[...], axis=0)
    column = lax.broadcasted_iota(jnp.int32, (8, TILE), 0)
    outs = []
    for s in range(8):
        pick = jnp.where(column == (codes[s] & 7), factor, 0.0)
        pick = jnp.sum(pick, axis=0, keepdims=True)
        ins[2 + s].wait()
        done[s] = inside[s] * pick
        outs.append(pltpu.make_async_copy(done.at[s], out.at[s], sem_out.at[s]))
        outs[-1].start()
    for copy in outs:
        copy.wait()


WHOLE = pl.BlockSpec(memory_space=pltpu.VMEM)
AWAY = pl.BlockSpec(memory_space=pl.ANY)
DENSE_LEFT = jax.ShapeDtypeStruct((8, 256, WIDE), BF16)
PRODUCT = jax.ShapeDtypeStruct((256, 1024), F32)
DENSE_RIGHT = pltpu.VMEM((1024, WIDE), BF16)
TILES = (8, TILE, TILE)


def cost(blocks):
    return pl.CostEstimate(
        flops=blocks * 2 * 256 * 1024 * 1024, bytes_accessed=blocks * 4 * 2**20, transcendentals=0
    )


def shards(tile_values, tile_coords, tile_counts, result_coords, result_counts):
    slot = jnp.arange(SLOTS, dtype=jnp.int32)
    at = tile_coords[0, 0]
    tile_code = jnp.where(slot < tile_counts[0, 0], at + (at >> 3), 8)
    slot = jnp.arange(8, dtype=jnp.int32)
    at = result_coords[0, 0]
    result_code = jnp.where(slot < result_counts[0, 0], at, at + 16)
    code = jnp.concatenate([tile_code, result_code, tile_code]).astype(BF16)
    unit = jnp.concatenate(
        [tile_values.reshape(BODY, TILE), jnp.broadcast_to(code[:, None], (16, TILE))]
    )

    def along(perm, v):
        return lax.ppermute(v, "loop", perm)

    def across(perm, v):
        return lax.ppermute(v, "group", perm)

    beside = along(YLO, unit)
    pair = jnp.concatenate([unit, along(CORE, unit)])
    beside_pair = along(CORE, beside)
    later, _ = lax.optimization_barrier((unit, beside))
    row = jnp.concatenate([later, across(YHI, later)])
    row = jnp.concatenate([row, across(XNEAR, row)])
    left = [row, across(XMIRROR, row)]

    streams = [pair, beside, beside_pair]
    right = [streams]
    for r in range(3):
        streams = [along(RING, v) for v in streams]
        right += [streams, [along(CORE, v) for v in streams]]
    last = [along(RING, v) for v in streams[:2]]
    last.append(along(CORE, last[1]))

    limit = pltpu.CompilerParams(vmem_limit_bytes=24 * 2**20)
    dense_left, product = pl.pallas_call(
        begin,
        in_specs=[WHOLE] * 17,
        out_specs=[WHOLE] * 2,
        out_shape=[DENSE_LEFT, PRODUCT],
        scratch_shapes=[DENSE_RIGHT],
        compiler_params=limit,
        cost_estimate=cost(6),
    )(*sum(right[:5], []), *left)
    product = pl.pallas_call(
        proceed,
        in_specs=[WHOLE] * 8,
        out_specs=WHOLE,
        out_shape=PRODUCT,
        scratch_shapes=[DENSE_RIGHT],
        compiler_params=limit,
        cost_estimate=cost(2),
    )(*sum(right[5:], []), dense_left, product)
    squares, sums = pl.pallas_call(
        finish,
        in_specs=[WHOLE] * 6,
        out_specs=[AWAY, WHOLE],
        out_shape=[jax.ShapeDtypeStruct(TILES, F32), jax.ShapeDtypeStruct((32, 8, TILE), F32)],
        scratch_shapes=[
            DENSE_RIGHT,
            pltpu.VMEM((256, 1024), F32),
            pltpu.VMEM(TILES, F32),
            pltpu.SemaphoreType.DMA((8,)),
        ],
        compiler_params=limit,
        cost_estimate=cost(1),
    )(unit, *last, dense_left, product)
    sums = lax.all_to_all(sums, "loop", 0, 0, tiled=True)
    out = pl.pallas_call(
        rescale,
        in_specs=[AWAY] * 3,
        out_specs=AWAY,
        out_shape=jax.ShapeDtypeStruct(TILES, F32),
        scratch_shapes=[
            pltpu.VMEM((16, TILE), BF16),
            pltpu.VMEM(TILES, F32),
            pltpu.VMEM((32, 8, TILE), F32),
            pltpu.VMEM(TILES, F32),
            pltpu.SemaphoreType.DMA((10,)),
            pltpu.SemaphoreType.DMA((8,)),
        ],
        compiler_params=limit,
    )(unit, squares, sums)
    return out[None, None]


def solution(mesh):
    placed = (
        P("loop", "group", None, None, None),
        P("loop", "group", None),
        P("loop", "group"),
        P("loop", "group", None),
        P("loop", "group"),
    )
    return jax.shard_map(
        shards,
        mesh=mesh,
        in_specs=placed,
        out_specs=P("loop", "group", None, None, None),
        check_vma=False,
    )
```

```python
import jax
import jax.numpy as jnp
from jax import lax
from jax.experimental import pallas as pl
from jax.experimental.pallas import tpu as pltpu
from jax.sharding import PartitionSpec as P

TILE = 128
SLOTS = 4
BODY = SLOTS * TILE
UNIT = BODY + 16
WIDE = 9 * TILE
F32, BF16 = jnp.float32, jnp.bfloat16


def loop_perm(f):
    pairs = []
    for i in range(32):
        z, y, c = f(i >> 2, (i >> 1) & 1, i & 1)
        pairs.append((i, (z % 8) * 4 + y * 2 + c))
    return pairs


def group_perm(f):
    pairs = []
    for i in range(8):
        x, y = f(i >> 1, i & 1)
        pairs.append((i, (x % 4) * 2 + y))
    return pairs


CORE = loop_perm(lambda z, y, c: (z, y, 1 - c))
YLO = loop_perm(lambda z, y, c: (z, 1 - y, c))
DIAGONAL = loop_perm(lambda z, y, c: (z, 1 - y, 1 - c))
RING = loop_perm(lambda z, y, c: (z + 1 - 2 * c, y, c))
YHI = group_perm(lambda x, y: (x, 1 - y))
XNEAR = group_perm(lambda x, y: (x ^ 1, y))
XMIRROR = group_perm(lambda x, y: (3 - x, y))


def scalars(ref, base, first, count):
    marks = ref[base : base + 16, :].astype(F32)
    return [jnp.max(marks[s : s + 1, :]).astype(jnp.int32) for s in range(first, first + count)]


def place(dst, ref, base, row):
    for s, code in enumerate(scalars(ref, base + BODY, 0, SLOTS)):
        r = (code >= 9).astype(jnp.int32)
        c = code - 9 * r
        rows = pl.ds(pl.multiple_of(row + r * TILE, TILE), TILE)
        cols = pl.ds(pl.multiple_of(c * TILE, TILE), TILE)
        dst[rows, cols] = ref[base + s * TILE : base + (s + 1) * TILE, :]


def where_am_i():
    i = lax.axis_index("loop")
    j = lax.axis_index("group")
    return i >> 2, (i >> 1) & 1, i & 1, j >> 1, j & 1


def multiply(dense_left, dense_right, j, units):
    dense_right[...] = jnp.zeros_like(dense_right)
    for ref, base, y, c in units:
        place(dense_right, ref, base, (y * 2 + c) * 256)
    return jnp.dot(
        dense_left[j, :, : 8 * TILE], dense_right[:, : 8 * TILE], preferred_element_type=F32
    )


def round_units(refs, y, c):
    pair, beside = refs
    return (
        (pair, 0, y, c),
        (pair, UNIT, y, 1 - c),
        (beside, 0, 1 - y, c),
        (beside, UNIT, 1 - y, 1 - c),
    )


def begin(*refs):
    own, rounds, left = refs[:2], refs[2:10], refs[10:12]
    dense_left, product, dense_right = refs[12:]
    z, y, c, x, h = where_am_i()
    dense_left[...] = jnp.zeros_like(dense_left)
    for k in range(8):
        xx = (x, x ^ 1, 3 - x, (3 - x) ^ 1)[k >> 1]
        place(dense_left.at[xx * 2 + (h ^ (k & 1))], left[k >> 2], (k & 3) * UNIT, 0)
    product[...] = multiply(dense_left, dense_right, z, round_units(own, y, c))
    sign = 1 - 2 * c
    for r in (1, 2):
        near, far = rounds[4 * r - 4 : 4 * r - 2], rounds[4 * r - 2 : 4 * r]
        product[...] += multiply(
            dense_left, dense_right, (z - sign * r) & 7, round_units(near, y, c)
        )
        product[...] += multiply(
            dense_left, dense_right, (z + sign * r) & 7, round_units(far, y, 1 - c)
        )


def proceed(*refs):
    near, far = refs[:2], refs[2:4]
    dense_left, before, product, dense_right = refs[4:]
    z, y, c, _, _ = where_am_i()
    sign = 1 - 2 * c
    product[...] = before[...] + multiply(
        dense_left, dense_right, (z - sign * 3) & 7, round_units(near, y, c)
    )
    product[...] += multiply(
        dense_left, dense_right, (z + sign * 3) & 7, round_units(far, y, 1 - c)
    )


def finish(codes, pair, beside, dense_left, before, squares, sums, dense_right, product, held, sem):
    z, y, c, _, _ = where_am_i()
    units = round_units((pair, beside), y, c)
    product[...] = before[...] + multiply(dense_left, dense_right, (z + 4) & 7, units)
    column = lax.broadcasted_iota(jnp.int32, (8, TILE), 0)
    total = jnp.zeros((8, TILE), F32)
    copies = []
    for s, code in enumerate(scalars(codes, 0, 0, 8)):
        used = code < 16
        p = code & 15
        rows = pl.ds(pl.multiple_of((p >> 3) * TILE, TILE), TILE)
        cols = pl.ds(pl.multiple_of((p & 7) * TILE, TILE), TILE)
        tile = product[rows, cols]
        tile = jnp.where(used, tile * tile, 0.0)
        held[s] = tile
        copies.append(pltpu.make_async_copy(held.at[s], squares.at[s], sem.at[s]))
        copies[-1].start()
        part = jnp.sum(tile, axis=0, keepdims=True)
        total += jnp.where(column == (p & 7), part, 0.0)
    for k in range(32):
        sums[k] = total
    for copy in copies:
        copy.wait()


def rescale(codes, squares, sums, out, marks, inside, parts, done, sem_in, sem_out):
    ins = [pltpu.make_async_copy(sums, parts, sem_in.at[8])]
    ins.append(pltpu.make_async_copy(codes, marks, sem_in.at[9]))
    ins += [pltpu.make_async_copy(squares.at[s], inside.at[s], sem_in.at[s]) for s in range(8)]
    for copy in ins:
        copy.start()
    ins[1].wait()
    at = scalars(marks, 0, 0, 8)
    ins[0].wait()
    factor = 8192.0 / jnp.sum(parts[...], axis=0)
    column = lax.broadcasted_iota(jnp.int32, (8, TILE), 0)
    outs = []
    for s in range(8):
        pick = jnp.where(column == (at[s] & 7), factor, 0.0)
        pick = jnp.sum(pick, axis=0, keepdims=True)
        ins[2 + s].wait()
        done[s] = inside[s] * pick
        outs.append(pltpu.make_async_copy(done.at[s], out.at[s], sem_out.at[s]))
        outs[-1].start()
    for copy in outs:
        copy.wait()


WHOLE = pl.BlockSpec(memory_space=pltpu.VMEM)
AWAY = pl.BlockSpec(memory_space=pl.ANY)
DENSE_LEFT = jax.ShapeDtypeStruct((8, 256, WIDE), BF16)
PRODUCT = jax.ShapeDtypeStruct((256, 1024), F32)
DENSE_RIGHT = pltpu.VMEM((1024, WIDE), BF16)
TILES = (8, TILE, TILE)


def cost(blocks):
    return pl.CostEstimate(
        flops=blocks * 2 * 256 * 1024 * 1024, bytes_accessed=blocks * 4 * 2**20, transcendentals=0
    )


def shards(tile_values, tile_coords, tile_counts, result_coords, result_counts):
    slot = jnp.arange(16, dtype=jnp.int32)
    at = jnp.pad(tile_coords[0, 0], (0, 12))
    code = jnp.where(slot < tile_counts[0, 0], at + (at >> 3), 8).astype(BF16)
    unit = jnp.concatenate(
        [tile_values.reshape(BODY, TILE), jnp.broadcast_to(code[:, None], (16, TILE))]
    )

    def along(perm, v):
        return lax.ppermute(v, "loop", perm)

    def across(perm, v):
        return lax.ppermute(v, "group", perm)

    beside, crossed = along(YLO, unit), along(DIAGONAL, unit)
    first = jnp.concatenate([unit, along(CORE, unit)])
    beside, crossed, _ = lax.optimization_barrier((beside, crossed, first))
    second = jnp.concatenate([beside, crossed])
    later, beside_later, _ = lax.optimization_barrier((unit, result_coords, beside))
    row = jnp.concatenate([later, across(YHI, later)])
    row = jnp.concatenate([row, across(XNEAR, row)])
    left = [row, across(XMIRROR, row)]
    at = jnp.pad(beside_later[0, 0], (0, 8))
    code = jnp.where(slot < result_counts[0, 0], at, at + 16).astype(BF16)
    codes = jnp.broadcast_to(code[:, None], (16, TILE))

    streams = [first, second]
    right = [streams]
    for r in range(3):
        streams = [along(RING, v) for v in streams]
        right += [streams, [along(CORE, v) for v in streams]]
    last = [along(RING, v) for v in streams]

    limit = pltpu.CompilerParams(vmem_limit_bytes=24 * 2**20)
    dense_left, product = pl.pallas_call(
        begin,
        in_specs=[WHOLE] * 12,
        out_specs=[WHOLE] * 2,
        out_shape=[DENSE_LEFT, PRODUCT],
        scratch_shapes=[DENSE_RIGHT],
        compiler_params=limit,
        cost_estimate=cost(6),
    )(*sum(right[:5], []), *left)
    product = pl.pallas_call(
        proceed,
        in_specs=[WHOLE] * 6,
        out_specs=WHOLE,
        out_shape=PRODUCT,
        scratch_shapes=[DENSE_RIGHT],
        compiler_params=limit,
        cost_estimate=cost(2),
    )(*sum(right[5:], []), dense_left, product)
    squares, sums = pl.pallas_call(
        finish,
        in_specs=[WHOLE] * 5,
        out_specs=[AWAY, WHOLE],
        out_shape=[jax.ShapeDtypeStruct(TILES, F32), jax.ShapeDtypeStruct((32, 8, TILE), F32)],
        scratch_shapes=[
            DENSE_RIGHT,
            pltpu.VMEM((256, 1024), F32),
            pltpu.VMEM(TILES, F32),
            pltpu.SemaphoreType.DMA((8,)),
        ],
        compiler_params=limit,
        cost_estimate=cost(1),
    )(codes, *last, dense_left, product)
    sums = lax.all_to_all(sums, "loop", 0, 0, tiled=True)
    out = pl.pallas_call(
        rescale,
        in_specs=[AWAY] * 3,
        out_specs=AWAY,
        out_shape=jax.ShapeDtypeStruct(TILES, F32),
        scratch_shapes=[
            pltpu.VMEM((16, TILE), BF16),
            pltpu.VMEM(TILES, F32),
            pltpu.VMEM((32, 8, TILE), F32),
            pltpu.VMEM(TILES, F32),
            pltpu.SemaphoreType.DMA((10,)),
            pltpu.SemaphoreType.DMA((8,)),
        ],
        compiler_params=limit,
    )(codes, squares, sums)
    return out[None, None]


def solution(mesh):
    placed = (
        P("loop", "group", None, None, None),
        P("loop", "group", None),
        P("loop", "group"),
        P("loop", "group", None),
        P("loop", "group"),
    )
    return jax.shard_map(
        shards,
        mesh=mesh,
        in_specs=placed,
        out_specs=P("loop", "group", None, None, None),
        check_vma=False,
    )
```

```python
import jax
import jax.numpy as jnp
from jax import lax
from jax.experimental import pallas as pl
from jax.experimental.pallas import tpu as pltpu
from jax.sharding import PartitionSpec as P

TILE = 128
SLOTS = 4
BODY = SLOTS * TILE
UNIT = BODY + 16
WIDE = 9 * TILE
F32, BF16 = jnp.float32, jnp.bfloat16


def loop_perm(f):
    pairs = []
    for i in range(32):
        z, y, c = f(i >> 2, (i >> 1) & 1, i & 1)
        pairs.append((i, (z % 8) * 4 + y * 2 + c))
    return pairs


def group_perm(f):
    pairs = []
    for i in range(8):
        x, y = f(i >> 1, i & 1)
        pairs.append((i, (x % 4) * 2 + y))
    return pairs


CORE = loop_perm(lambda z, y, c: (z, y, 1 - c))
YLO = loop_perm(lambda z, y, c: (z, 1 - y, c))
DIAGONAL = loop_perm(lambda z, y, c: (z, 1 - y, 1 - c))
RING = loop_perm(lambda z, y, c: (z + 1 - 2 * c, y, c))
YHI = group_perm(lambda x, y: (x, 1 - y))
XNEAR = group_perm(lambda x, y: (x ^ 1, y))
XMIRROR = group_perm(lambda x, y: (3 - x, y))


def scalars(ref, base, first, count):
    marks = ref[base : base + 16, :].astype(F32)
    return [jnp.max(marks[s : s + 1, :]).astype(jnp.int32) for s in range(first, first + count)]


def place(dst, ref, base, row):
    for s, code in enumerate(scalars(ref, base + BODY, 0, SLOTS)):
        r = (code >= 9).astype(jnp.int32)
        c = code - 9 * r
        rows = pl.ds(pl.multiple_of(row + r * TILE, TILE), TILE)
        cols = pl.ds(pl.multiple_of(c * TILE, TILE), TILE)
        dst[rows, cols] = ref[base + s * TILE : base + (s + 1) * TILE, :]


def where_am_i():
    i = lax.axis_index("loop")
    j = lax.axis_index("group")
    return i >> 2, (i >> 1) & 1, i & 1, j >> 1, j & 1


def multiply(dense_left, dense_right, j, units):
    dense_right[...] = jnp.zeros_like(dense_right)
    for ref, base, y, c in units:
        place(dense_right, ref, base, (y * 2 + c) * 256)
    return jnp.dot(
        dense_left[j, :, : 8 * TILE], dense_right[:, : 8 * TILE], preferred_element_type=F32
    )


def round_units(refs, y, c):
    pair, beside = refs
    return (
        (pair, 0, y, c),
        (pair, UNIT, y, 1 - c),
        (beside, 0, 1 - y, c),
        (beside, UNIT, 1 - y, 1 - c),
    )


def begin(*refs):
    own, rounds, left = refs[:2], refs[2:10], refs[10:12]
    dense_left, product, dense_right = refs[12:]
    z, y, c, x, h = where_am_i()
    dense_left[...] = jnp.zeros_like(dense_left)
    for k in range(8):
        xx = (x, x ^ 1, 3 - x, (3 - x) ^ 1)[k >> 1]
        place(dense_left.at[xx * 2 + (h ^ (k & 1))], left[k >> 2], (k & 3) * UNIT, 0)
    product[...] = multiply(dense_left, dense_right, z, round_units(own, y, c))
    sign = 1 - 2 * c
    for r in (1, 2):
        near, far = rounds[4 * r - 4 : 4 * r - 2], rounds[4 * r - 2 : 4 * r]
        product[...] += multiply(
            dense_left, dense_right, (z - sign * r) & 7, round_units(near, y, c)
        )
        product[...] += multiply(
            dense_left, dense_right, (z + sign * r) & 7, round_units(far, y, 1 - c)
        )


def proceed(*refs):
    near, far = refs[:2], refs[2:4]
    dense_left, before, product, dense_right = refs[4:]
    z, y, c, _, _ = where_am_i()
    sign = 1 - 2 * c
    product[...] = before[...] + multiply(
        dense_left, dense_right, (z - sign * 3) & 7, round_units(near, y, c)
    )
    product[...] += multiply(
        dense_left, dense_right, (z + sign * 3) & 7, round_units(far, y, 1 - c)
    )


def finish(codes, pair, beside, dense_left, before, squares, sums, dense_right, product, held, sem):
    z, y, c, _, _ = where_am_i()
    units = round_units((pair, beside), y, c)
    product[...] = before[...] + multiply(dense_left, dense_right, (z + 4) & 7, units)
    column = lax.broadcasted_iota(jnp.int32, (8, TILE), 0)
    total = jnp.zeros((8, TILE), F32)
    copies = []
    for s, code in enumerate(scalars(codes, 0, 0, 8)):
        used = code < 16
        p = code & 15
        rows = pl.ds(pl.multiple_of((p >> 3) * TILE, TILE), TILE)
        cols = pl.ds(pl.multiple_of((p & 7) * TILE, TILE), TILE)
        tile = product[rows, cols]
        tile = jnp.where(used, tile * tile, 0.0)
        held[s] = tile
        copies.append(pltpu.make_async_copy(held.at[s], squares.at[s], sem.at[s]))
        copies[-1].start()
        part = jnp.sum(tile, axis=0, keepdims=True)
        total += jnp.where(column == (p & 7), part, 0.0)
    for k in range(32):
        sums[k] = total
    for copy in copies:
        copy.wait()


def rescale(codes, squares, sums, out, marks, inside, parts, done, sem_in, sem_out):
    ins = [pltpu.make_async_copy(sums, parts, sem_in.at[8])]
    ins.append(pltpu.make_async_copy(codes, marks, sem_in.at[9]))
    ins += [pltpu.make_async_copy(squares.at[s], inside.at[s], sem_in.at[s]) for s in range(8)]
    for copy in ins:
        copy.start()
    ins[1].wait()
    at = scalars(marks, 0, 0, 8)
    ins[0].wait()
    factor = 8192.0 / jnp.sum(parts[...], axis=0)
    column = lax.broadcasted_iota(jnp.int32, (8, TILE), 0)
    outs = []
    for s in range(8):
        pick = jnp.where(column == (at[s] & 7), factor, 0.0)
        pick = jnp.sum(pick, axis=0, keepdims=True)
        ins[2 + s].wait()
        done[s] = inside[s] * pick
        outs.append(pltpu.make_async_copy(done.at[s], out.at[s], sem_out.at[s]))
        outs[-1].start()
    for copy in outs:
        copy.wait()


WHOLE = pl.BlockSpec(memory_space=pltpu.VMEM)
AWAY = pl.BlockSpec(memory_space=pl.ANY)
DENSE_LEFT = jax.ShapeDtypeStruct((8, 256, WIDE), BF16)
PRODUCT = jax.ShapeDtypeStruct((256, 1024), F32)
DENSE_RIGHT = pltpu.VMEM((1024, WIDE), BF16)
TILES = (8, TILE, TILE)


def cost(blocks):
    return pl.CostEstimate(
        flops=blocks * 2 * 256 * 1024 * 1024, bytes_accessed=blocks * 4 * 2**20, transcendentals=0
    )


def shards(tile_values, tile_coords, tile_counts, result_coords, result_counts):
    slot = jnp.arange(16, dtype=jnp.int32)
    at = jnp.pad(tile_coords[0, 0], (0, 12))
    code = jnp.where(slot < tile_counts[0, 0], at + (at >> 3), 8).astype(BF16)
    unit = jnp.concatenate(
        [tile_values.reshape(BODY, TILE), jnp.broadcast_to(code[:, None], (16, TILE))]
    )

    def along(perm, v):
        return lax.ppermute(v, "loop", perm)

    def across(perm, v):
        return lax.ppermute(v, "group", perm)

    beside, crossed = along(YLO, unit), along(DIAGONAL, unit)
    first = jnp.concatenate([unit, along(CORE, unit)])
    beside, crossed, _ = lax.optimization_barrier((beside, crossed, first))
    second = jnp.concatenate([beside, crossed])
    later, beside_later, _ = lax.optimization_barrier((unit, result_coords, first))
    row = jnp.concatenate([later, across(YHI, later)])
    row = jnp.concatenate([row, across(XNEAR, row)])
    left = [row, across(XMIRROR, row)]
    at = jnp.pad(beside_later[0, 0], (0, 8))
    code = jnp.where(slot < result_counts[0, 0], at, at + 16).astype(BF16)
    codes = jnp.broadcast_to(code[:, None], (16, TILE))

    streams = [first, second]
    right = [streams]
    for r in range(3):
        ahead = along(RING, streams[0])
        behind = streams[1]
        if r == 0:
            behind, _ = lax.optimization_barrier((behind, ahead))
        streams = [ahead, along(RING, behind)]
        right += [streams, [along(CORE, v) for v in streams]]
    last = [along(RING, v) for v in streams]

    limit = pltpu.CompilerParams(vmem_limit_bytes=24 * 2**20)
    dense_left, product = pl.pallas_call(
        begin,
        in_specs=[WHOLE] * 12,
        out_specs=[WHOLE] * 2,
        out_shape=[DENSE_LEFT, PRODUCT],
        scratch_shapes=[DENSE_RIGHT],
        compiler_params=limit,
        cost_estimate=cost(6),
    )(*sum(right[:5], []), *left)
    product = pl.pallas_call(
        proceed,
        in_specs=[WHOLE] * 6,
        out_specs=WHOLE,
        out_shape=PRODUCT,
        scratch_shapes=[DENSE_RIGHT],
        compiler_params=limit,
        cost_estimate=cost(2),
    )(*sum(right[5:], []), dense_left, product)
    squares, sums = pl.pallas_call(
        finish,
        in_specs=[WHOLE] * 5,
        out_specs=[AWAY, WHOLE],
        out_shape=[jax.ShapeDtypeStruct(TILES, F32), jax.ShapeDtypeStruct((32, 8, TILE), F32)],
        scratch_shapes=[
            DENSE_RIGHT,
            pltpu.VMEM((256, 1024), F32),
            pltpu.VMEM(TILES, F32),
            pltpu.SemaphoreType.DMA((8,)),
        ],
        compiler_params=limit,
        cost_estimate=cost(1),
    )(codes, *last, dense_left, product)
    sums = lax.all_to_all(sums, "loop", 0, 0, tiled=True)
    out = pl.pallas_call(
        rescale,
        in_specs=[AWAY] * 3,
        out_specs=AWAY,
        out_shape=jax.ShapeDtypeStruct(TILES, F32),
        scratch_shapes=[
            pltpu.VMEM((16, TILE), BF16),
            pltpu.VMEM(TILES, F32),
            pltpu.VMEM((32, 8, TILE), F32),
            pltpu.VMEM(TILES, F32),
            pltpu.SemaphoreType.DMA((10,)),
            pltpu.SemaphoreType.DMA((8,)),
        ],
        compiler_params=limit,
    )(codes, squares, sums)
    return out[None, None]


def solution(mesh):
    placed = (
        P("loop", "group", None, None, None),
        P("loop", "group", None),
        P("loop", "group"),
        P("loop", "group", None),
        P("loop", "group"),
    )
    return jax.shard_map(
        shards,
        mesh=mesh,
        in_specs=placed,
        out_specs=P("loop", "group", None, None, None),
        check_vma=False,
    )
```

```python
import jax
import jax.numpy as jnp
from jax import lax
from jax.experimental import pallas as pl
from jax.experimental.pallas import tpu as pltpu
from jax.sharding import PartitionSpec as P

TILE = 128
SLOTS = 4
BODY = SLOTS * TILE
UNIT = BODY + 16
WIDE = 9 * TILE
F32, BF16 = jnp.float32, jnp.bfloat16


def loop_perm(f):
    pairs = []
    for i in range(32):
        z, y, c = f(i >> 2, (i >> 1) & 1, i & 1)
        pairs.append((i, (z % 8) * 4 + y * 2 + c))
    return pairs


def group_perm(f):
    pairs = []
    for i in range(8):
        x, y = f(i >> 1, i & 1)
        pairs.append((i, (x % 4) * 2 + y))
    return pairs


CORE = loop_perm(lambda z, y, c: (z, y, 1 - c))
YLO = loop_perm(lambda z, y, c: (z, 1 - y, c))
DIAGONAL = loop_perm(lambda z, y, c: (z, 1 - y, 1 - c))
RING = loop_perm(lambda z, y, c: (z + 1 - 2 * c, y, c))
YHI = group_perm(lambda x, y: (x, 1 - y))
XNEAR = group_perm(lambda x, y: (x ^ 1, y))
XMIRROR = group_perm(lambda x, y: (3 - x, y))


def scalars(ref, base, first, count):
    marks = ref[base : base + 16, :].astype(F32)
    return [jnp.max(marks[s : s + 1, :]).astype(jnp.int32) for s in range(first, first + count)]


def place(dst, ref, base, row):
    for s, code in enumerate(scalars(ref, base + BODY, 0, SLOTS)):
        r = (code >= 9).astype(jnp.int32)
        c = code - 9 * r
        rows = pl.ds(pl.multiple_of(row + r * TILE, TILE), TILE)
        cols = pl.ds(pl.multiple_of(c * TILE, TILE), TILE)
        dst[rows, cols] = ref[base + s * TILE : base + (s + 1) * TILE, :]


def where_am_i():
    i = lax.axis_index("loop")
    j = lax.axis_index("group")
    return i >> 2, (i >> 1) & 1, i & 1, j >> 1, j & 1


def multiply(dense_left, dense_right, j, units):
    dense_right[...] = jnp.zeros_like(dense_right)
    for ref, base, y, c in units:
        place(dense_right, ref, base, (y * 2 + c) * 256)
    return jnp.dot(
        dense_left[j, :, : 8 * TILE], dense_right[:, : 8 * TILE], preferred_element_type=F32
    )


def round_units(refs, y, c):
    beside, pair = refs
    return (
        (pair, 0, y, c),
        (pair, UNIT, y, 1 - c),
        (beside, 0, 1 - y, c),
        (beside, UNIT, 1 - y, 1 - c),
    )


def begin(*refs):
    own, rounds, left = refs[:2], refs[2:10], refs[10:12]
    dense_left, product, dense_right = refs[12:]
    z, y, c, x, h = where_am_i()
    dense_left[...] = jnp.zeros_like(dense_left)
    for k in range(8):
        xx = (x, x ^ 1, 3 - x, (3 - x) ^ 1)[k >> 1]
        place(dense_left.at[xx * 2 + (h ^ (k & 1))], left[k >> 2], (k & 3) * UNIT, 0)
    product[...] = multiply(dense_left, dense_right, z, round_units(own, y, c))
    sign = 1 - 2 * c
    for r in (1, 2):
        near, far = rounds[4 * r - 4 : 4 * r - 2], rounds[4 * r - 2 : 4 * r]
        product[...] += multiply(
            dense_left, dense_right, (z - sign * r) & 7, round_units(near, y, c)
        )
        product[...] += multiply(
            dense_left, dense_right, (z + sign * r) & 7, round_units(far, y, 1 - c)
        )


def proceed(*refs):
    near, far = refs[:2], refs[2:4]
    dense_left, before, product, dense_right = refs[4:]
    z, y, c, _, _ = where_am_i()
    sign = 1 - 2 * c
    product[...] = before[...] + multiply(
        dense_left, dense_right, (z - sign * 3) & 7, round_units(near, y, c)
    )
    product[...] += multiply(
        dense_left, dense_right, (z + sign * 3) & 7, round_units(far, y, 1 - c)
    )


def finish(codes, beside, pair, dense_left, before, squares, sums, dense_right, product, held, sem):
    z, y, c, _, _ = where_am_i()
    units = round_units((beside, pair), y, c)
    product[...] = before[...] + multiply(dense_left, dense_right, (z + 4) & 7, units)
    column = lax.broadcasted_iota(jnp.int32, (8, TILE), 0)
    total = jnp.zeros((8, TILE), F32)
    copies = []
    for s, code in enumerate(scalars(codes, 0, 0, 8)):
        used = code < 16
        p = code & 15
        rows = pl.ds(pl.multiple_of((p >> 3) * TILE, TILE), TILE)
        cols = pl.ds(pl.multiple_of((p & 7) * TILE, TILE), TILE)
        tile = product[rows, cols]
        tile = jnp.where(used, tile * tile, 0.0)
        held[s] = tile
        copies.append(pltpu.make_async_copy(held.at[s], squares.at[s], sem.at[s]))
        copies[-1].start()
        part = jnp.sum(tile, axis=0, keepdims=True)
        total += jnp.where(column == (p & 7), part, 0.0)
    for k in range(32):
        sums[k] = total
    for copy in copies:
        copy.wait()


def rescale(codes, squares, sums, out, marks, inside, parts, done, sem_in, sem_out):
    ins = [pltpu.make_async_copy(sums, parts, sem_in.at[8])]
    ins.append(pltpu.make_async_copy(codes, marks, sem_in.at[9]))
    ins += [pltpu.make_async_copy(squares.at[s], inside.at[s], sem_in.at[s]) for s in range(8)]
    for copy in ins:
        copy.start()
    ins[1].wait()
    at = scalars(marks, 0, 0, 8)
    ins[0].wait()
    factor = 8192.0 / jnp.sum(parts[...], axis=0)
    column = lax.broadcasted_iota(jnp.int32, (8, TILE), 0)
    outs = []
    for s in range(8):
        pick = jnp.where(column == (at[s] & 7), factor, 0.0)
        pick = jnp.sum(pick, axis=0, keepdims=True)
        ins[2 + s].wait()
        done[s] = inside[s] * pick
        outs.append(pltpu.make_async_copy(done.at[s], out.at[s], sem_out.at[s]))
        outs[-1].start()
    for copy in outs:
        copy.wait()


WHOLE = pl.BlockSpec(memory_space=pltpu.VMEM)
AWAY = pl.BlockSpec(memory_space=pl.ANY)
DENSE_LEFT = jax.ShapeDtypeStruct((8, 256, WIDE), BF16)
PRODUCT = jax.ShapeDtypeStruct((256, 1024), F32)
DENSE_RIGHT = pltpu.VMEM((1024, WIDE), BF16)
TILES = (8, TILE, TILE)


def cost(blocks):
    return pl.CostEstimate(
        flops=blocks * 2 * 256 * 1024 * 1024, bytes_accessed=blocks * 4 * 2**20, transcendentals=0
    )


def shards(tile_values, tile_coords, tile_counts, result_coords, result_counts):
    slot = jnp.arange(16, dtype=jnp.int32)
    at = jnp.pad(tile_coords[0, 0], (0, 12))
    code = jnp.where(slot < tile_counts[0, 0], at + (at >> 3), 8).astype(BF16)
    unit = jnp.concatenate(
        [tile_values.reshape(BODY, TILE), jnp.broadcast_to(code[:, None], (16, TILE))]
    )

    def along(perm, v):
        return lax.ppermute(v, "loop", perm)

    def across(perm, v):
        return lax.ppermute(v, "group", perm)

    beside, crossed = along(YLO, unit), along(DIAGONAL, unit)
    first = jnp.concatenate([unit, along(CORE, unit)])
    beside, crossed, _ = lax.optimization_barrier((beside, crossed, first))
    second = jnp.concatenate([beside, crossed])
    later, beside_later, _ = lax.optimization_barrier((unit, result_coords, first))
    row = jnp.concatenate([later, across(YHI, later)])
    row = jnp.concatenate([row, across(XNEAR, row)])
    left = [row, across(XMIRROR, row)]
    at = jnp.pad(beside_later[0, 0], (0, 8))
    code = jnp.where(slot < result_counts[0, 0], at, at + 16).astype(BF16)
    codes = jnp.broadcast_to(code[:, None], (16, TILE))

    streams = [second, first]
    right = [streams]
    for r in range(3):
        streams = [along(RING, v) for v in streams]
        other = lax.optimization_barrier(streams)
        right += [streams, [along(CORE, v) for v in other]]
    last = [along(RING, v) for v in streams]

    limit = pltpu.CompilerParams(vmem_limit_bytes=24 * 2**20)
    dense_left, product = pl.pallas_call(
        begin,
        in_specs=[WHOLE] * 12,
        out_specs=[WHOLE] * 2,
        out_shape=[DENSE_LEFT, PRODUCT],
        scratch_shapes=[DENSE_RIGHT],
        compiler_params=limit,
        cost_estimate=cost(6),
    )(*sum(right[:5], []), *left)
    product = pl.pallas_call(
        proceed,
        in_specs=[WHOLE] * 6,
        out_specs=WHOLE,
        out_shape=PRODUCT,
        scratch_shapes=[DENSE_RIGHT],
        compiler_params=limit,
        cost_estimate=cost(2),
    )(*sum(right[5:], []), dense_left, product)
    squares, sums = pl.pallas_call(
        finish,
        in_specs=[WHOLE] * 5,
        out_specs=[AWAY, WHOLE],
        out_shape=[jax.ShapeDtypeStruct(TILES, F32), jax.ShapeDtypeStruct((32, 8, TILE), F32)],
        scratch_shapes=[
            DENSE_RIGHT,
            pltpu.VMEM((256, 1024), F32),
            pltpu.VMEM(TILES, F32),
            pltpu.SemaphoreType.DMA((8,)),
        ],
        compiler_params=limit,
        cost_estimate=cost(1),
    )(codes, *last, dense_left, product)
    sums = lax.all_to_all(sums, "loop", 0, 0, tiled=True)
    out = pl.pallas_call(
        rescale,
        in_specs=[AWAY] * 3,
        out_specs=AWAY,
        out_shape=jax.ShapeDtypeStruct(TILES, F32),
        scratch_shapes=[
            pltpu.VMEM((16, TILE), BF16),
            pltpu.VMEM(TILES, F32),
            pltpu.VMEM((32, 8, TILE), F32),
            pltpu.VMEM(TILES, F32),
            pltpu.SemaphoreType.DMA((10,)),
            pltpu.SemaphoreType.DMA((8,)),
        ],
        compiler_params=limit,
    )(codes, squares, sums)
    return out[None, None]


def solution(mesh):
    placed = (
        P("loop", "group", None, None, None),
        P("loop", "group", None),
        P("loop", "group"),
        P("loop", "group", None),
        P("loop", "group"),
    )
    return jax.shard_map(
        shards,
        mesh=mesh,
        in_specs=placed,
        out_specs=P("loop", "group", None, None, None),
        check_vma=False,
    )
```

```python
import jax
import jax.numpy as jnp
from jax import lax
from jax.experimental import pallas as pl
from jax.experimental.pallas import tpu as pltpu
from jax.sharding import PartitionSpec as P

TILE = 128
SLOTS = 4
BODY = SLOTS * TILE
UNIT = BODY + 16
WIDE = 9 * TILE
F32, BF16 = jnp.float32, jnp.bfloat16


def loop_perm(f):
    pairs = []
    for i in range(32):
        z, y, c = f(i >> 2, (i >> 1) & 1, i & 1)
        pairs.append((i, (z % 8) * 4 + y * 2 + c))
    return pairs


def group_perm(f):
    pairs = []
    for i in range(8):
        x, y = f(i >> 1, i & 1)
        pairs.append((i, (x % 4) * 2 + y))
    return pairs


CORE = loop_perm(lambda z, y, c: (z, y, 1 - c))
YLO = loop_perm(lambda z, y, c: (z, 1 - y, c))
DIAGONAL = loop_perm(lambda z, y, c: (z, 1 - y, 1 - c))
RING = loop_perm(lambda z, y, c: (z + 1 - 2 * c, y, c))
YHI = group_perm(lambda x, y: (x, 1 - y))
XNEAR = group_perm(lambda x, y: (x ^ 1, y))
XMIRROR = group_perm(lambda x, y: (3 - x, y))


def scalars(ref, base, first, count):
    marks = ref[base : base + 16, :].astype(F32)
    return [jnp.max(marks[s : s + 1, :]).astype(jnp.int32) for s in range(first, first + count)]


def place(dst, ref, base, row):
    for s, code in enumerate(scalars(ref, base + BODY, 0, SLOTS)):
        r = (code >= 9).astype(jnp.int32)
        c = code - 9 * r
        rows = pl.ds(pl.multiple_of(row + r * TILE, TILE), TILE)
        cols = pl.ds(pl.multiple_of(c * TILE, TILE), TILE)
        dst[rows, cols] = ref[base + s * TILE : base + (s + 1) * TILE, :]


def where_am_i():
    i = lax.axis_index("loop")
    j = lax.axis_index("group")
    return i >> 2, (i >> 1) & 1, i & 1, j >> 1, j & 1


def multiply(dense_left, dense_right, j, units):
    dense_right[...] = jnp.zeros_like(dense_right)
    for ref, base, y, c in units:
        place(dense_right, ref, base, (y * 2 + c) * 256)
    return jnp.dot(
        dense_left[j, :, : 8 * TILE], dense_right[:, : 8 * TILE], preferred_element_type=F32
    )


def round_units(refs, y, c):
    beside, pair = refs
    return (
        (pair, 0, y, c),
        (pair, UNIT, y, 1 - c),
        (beside, 0, 1 - y, c),
        (beside, UNIT, 1 - y, 1 - c),
    )


def begin(*refs):
    own, rounds, left = refs[:2], refs[2:10], refs[10:12]
    dense_left, product, dense_right = refs[12:]
    z, y, c, x, h = where_am_i()
    dense_left[...] = jnp.zeros_like(dense_left)
    for k in range(8):
        xx = (x, x ^ 1, 3 - x, (3 - x) ^ 1)[k >> 1]
        place(dense_left.at[xx * 2 + (h ^ (k & 1))], left[k >> 2], (k & 3) * UNIT, 0)
    product[...] = multiply(dense_left, dense_right, z, round_units(own, y, c))
    sign = 1 - 2 * c
    for r in (1, 2):
        near, far = rounds[4 * r - 4 : 4 * r - 2], rounds[4 * r - 2 : 4 * r]
        product[...] += multiply(
            dense_left, dense_right, (z - sign * r) & 7, round_units(near, y, c)
        )
        product[...] += multiply(
            dense_left, dense_right, (z + sign * r) & 7, round_units(far, y, 1 - c)
        )


def proceed(*refs):
    near, far = refs[:2], refs[2:4]
    dense_left, before, product, dense_right = refs[4:]
    z, y, c, _, _ = where_am_i()
    sign = 1 - 2 * c
    product[...] = before[...] + multiply(
        dense_left, dense_right, (z - sign * 3) & 7, round_units(near, y, c)
    )
    product[...] += multiply(
        dense_left, dense_right, (z + sign * 3) & 7, round_units(far, y, 1 - c)
    )


def half(ref, y, c, dense_left, dense_half):
    z = where_am_i()[0]
    dense_half[...] = jnp.zeros_like(dense_half)
    place(dense_half, ref, 0, c * 256)
    place(dense_half, ref, UNIT, (1 - c) * 256)
    return jnp.dot(
        dense_left[(z + 4) & 7, :, pl.ds(pl.multiple_of(y * 512, 512), 512)],
        dense_half[:, : 8 * TILE],
        preferred_element_type=F32,
    )


def add_half(beside, dense_left, before, product, dense_half):
    _, y, c, _, _ = where_am_i()
    product[...] = before[...] + half(beside, 1 - y, c, dense_left, dense_half)


def finish(codes, pair, dense_left, before, squares, sums, dense_half, product, held, sem):
    _, y, c, _, _ = where_am_i()
    product[...] = before[...] + half(pair, y, c, dense_left, dense_half)
    column = lax.broadcasted_iota(jnp.int32, (8, TILE), 0)
    total = jnp.zeros((8, TILE), F32)
    copies = []
    for s, code in enumerate(scalars(codes, 0, 0, 8)):
        used = code < 16
        p = code & 15
        rows = pl.ds(pl.multiple_of((p >> 3) * TILE, TILE), TILE)
        cols = pl.ds(pl.multiple_of((p & 7) * TILE, TILE), TILE)
        tile = product[rows, cols]
        tile = jnp.where(used, tile * tile, 0.0)
        held[s] = tile
        copies.append(pltpu.make_async_copy(held.at[s], squares.at[s], sem.at[s]))
        copies[-1].start()
        part = jnp.sum(tile, axis=0, keepdims=True)
        total += jnp.where(column == (p & 7), part, 0.0)
    for k in range(32):
        sums[k] = total
    for copy in copies:
        copy.wait()


def rescale(codes, squares, sums, out, marks, inside, parts, done, sem_in, sem_out):
    ins = [pltpu.make_async_copy(sums, parts, sem_in.at[8])]
    ins.append(pltpu.make_async_copy(codes, marks, sem_in.at[9]))
    ins += [pltpu.make_async_copy(squares.at[s], inside.at[s], sem_in.at[s]) for s in range(8)]
    for copy in ins:
        copy.start()
    ins[1].wait()
    at = scalars(marks, 0, 0, 8)
    ins[0].wait()
    factor = 8192.0 / jnp.sum(parts[...], axis=0)
    column = lax.broadcasted_iota(jnp.int32, (8, TILE), 0)
    outs = []
    for s in range(8):
        pick = jnp.where(column == (at[s] & 7), factor, 0.0)
        pick = jnp.sum(pick, axis=0, keepdims=True)
        ins[2 + s].wait()
        done[s] = inside[s] * pick
        outs.append(pltpu.make_async_copy(done.at[s], out.at[s], sem_out.at[s]))
        outs[-1].start()
    for copy in outs:
        copy.wait()


WHOLE = pl.BlockSpec(memory_space=pltpu.VMEM)
AWAY = pl.BlockSpec(memory_space=pl.ANY)
DENSE_LEFT = jax.ShapeDtypeStruct((8, 256, WIDE), BF16)
PRODUCT = jax.ShapeDtypeStruct((256, 1024), F32)
DENSE_RIGHT = pltpu.VMEM((1024, WIDE), BF16)
DENSE_HALF = pltpu.VMEM((512, WIDE), BF16)
TILES = (8, TILE, TILE)


def cost(blocks):
    return pl.CostEstimate(
        flops=blocks * 2**20, bytes_accessed=blocks * 2**16, transcendentals=0
    )


def shards(tile_values, tile_coords, tile_counts, result_coords, result_counts):
    slot = jnp.arange(16, dtype=jnp.int32)
    at = jnp.pad(tile_coords[0, 0], (0, 12))
    code = jnp.where(slot < tile_counts[0, 0], at + (at >> 3), 8).astype(BF16)
    unit = jnp.concatenate(
        [tile_values.reshape(BODY, TILE), jnp.broadcast_to(code[:, None], (16, TILE))]
    )

    def along(perm, v):
        return lax.ppermute(v, "loop", perm)

    def across(perm, v):
        return lax.ppermute(v, "group", perm)

    beside, crossed = along(YLO, unit), along(DIAGONAL, unit)
    pair = along(CORE, unit)
    first = jnp.concatenate([unit, pair])
    beside, crossed, _ = lax.optimization_barrier((beside, crossed, first))
    second = jnp.concatenate([beside, crossed])
    later, beside_later, _ = lax.optimization_barrier((unit, result_coords, pair))
    row = jnp.concatenate([later, across(YHI, later)])
    at = jnp.pad(beside_later[0, 0], (0, 8))
    code = jnp.where(slot < result_counts[0, 0], at, at + 16).astype(BF16)
    codes = jnp.broadcast_to(code[:, None], (16, TILE))

    def after(v, *others):
        return lax.optimization_barrier((v, *others))

    streams = [second, first]
    right = [streams]
    row = jnp.concatenate([row, across(XNEAR, row)])
    for r in range(3):
        if r == 2:
            streams = [after(streams[0], *right[-3])[0], streams[1]]
        streams = [along(RING, v) for v in streams]
        if r == 0:
            streams[1], row = after(streams[1], row)
            left = [row, across(XMIRROR, row)]
        other = after(*streams)
        if r == 2:
            other = after(*other, left[1])[:2]
        right += [streams, [along(CORE, v) for v in other]]
    streams = [after(streams[0], *right[-3])[0], streams[1]]
    last = [along(RING, v) for v in streams]

    limit = pltpu.CompilerParams(vmem_limit_bytes=24 * 2**20)
    dense_left, product = pl.pallas_call(
        begin,
        in_specs=[WHOLE] * 12,
        out_specs=[WHOLE] * 2,
        out_shape=[DENSE_LEFT, PRODUCT],
        scratch_shapes=[DENSE_RIGHT],
        compiler_params=limit,
        cost_estimate=cost(6),
    )(*sum(right[:5], []), *left)
    product = pl.pallas_call(
        add_half,
        in_specs=[WHOLE] * 3,
        out_specs=WHOLE,
        out_shape=PRODUCT,
        scratch_shapes=[DENSE_HALF],
        compiler_params=limit,
        cost_estimate=cost(1),
    )(last[0], dense_left, product)
    product = pl.pallas_call(
        proceed,
        in_specs=[WHOLE] * 6,
        out_specs=WHOLE,
        out_shape=PRODUCT,
        scratch_shapes=[DENSE_RIGHT],
        compiler_params=limit,
        cost_estimate=cost(2),
    )(*sum(right[5:], []), dense_left, product)
    squares, sums = pl.pallas_call(
        finish,
        in_specs=[WHOLE] * 4,
        out_specs=[AWAY, WHOLE],
        out_shape=[jax.ShapeDtypeStruct(TILES, F32), jax.ShapeDtypeStruct((32, 8, TILE), F32)],
        scratch_shapes=[
            DENSE_HALF,
            pltpu.VMEM((256, 1024), F32),
            pltpu.VMEM(TILES, F32),
            pltpu.SemaphoreType.DMA((8,)),
        ],
        compiler_params=limit,
        cost_estimate=cost(1),
    )(codes, last[1], dense_left, product)
    sums = lax.all_to_all(sums, "loop", 0, 0, tiled=True)
    out = pl.pallas_call(
        rescale,
        in_specs=[AWAY] * 3,
        out_specs=AWAY,
        out_shape=jax.ShapeDtypeStruct(TILES, F32),
        scratch_shapes=[
            pltpu.VMEM((16, TILE), BF16),
            pltpu.VMEM(TILES, F32),
            pltpu.VMEM((32, 8, TILE), F32),
            pltpu.VMEM(TILES, F32),
            pltpu.SemaphoreType.DMA((10,)),
            pltpu.SemaphoreType.DMA((8,)),
        ],
        compiler_params=limit,
    )(codes, squares, sums)
    return out[None, None]


def solution(mesh):
    placed = (
        P("loop", "group", None, None, None),
        P("loop", "group", None),
        P("loop", "group"),
        P("loop", "group", None),
        P("loop", "group"),
    )
    return jax.shard_map(
        shards,
        mesh=mesh,
        in_specs=placed,
        out_specs=P("loop", "group", None, None, None),
        check_vma=False,
    )
```

```python
import jax
import jax.numpy as jnp
from jax import lax
from jax.experimental import pallas as pl
from jax.experimental.pallas import tpu as pltpu
from jax.sharding import PartitionSpec as P

TILE = 128
SLOTS = 4
BODY = SLOTS * TILE
UNIT = BODY + 16
WIDE = 9 * TILE
F32, BF16 = jnp.float32, jnp.bfloat16


def loop_perm(f):
    pairs = []
    for i in range(32):
        z, y, c = f(i >> 2, (i >> 1) & 1, i & 1)
        pairs.append((i, (z % 8) * 4 + y * 2 + c))
    return pairs


def group_perm(f):
    pairs = []
    for i in range(8):
        x, y = f(i >> 1, i & 1)
        pairs.append((i, (x % 4) * 2 + y))
    return pairs


CORE = loop_perm(lambda z, y, c: (z, y, 1 - c))
YLO = loop_perm(lambda z, y, c: (z, 1 - y, c))
DIAGONAL = loop_perm(lambda z, y, c: (z, 1 - y, 1 - c))
RING = loop_perm(lambda z, y, c: (z + 1 - 2 * c, y, c))
YHI = group_perm(lambda x, y: (x, 1 - y))
XNEAR = group_perm(lambda x, y: (x ^ 1, y))
XMIRROR = group_perm(lambda x, y: (3 - x, y))


def scalars(ref, base, first, count):
    marks = ref[base : base + 16, :].astype(F32)
    return [jnp.max(marks[s : s + 1, :]).astype(jnp.int32) for s in range(first, first + count)]


def place(dst, ref, base, row):
    for s, code in enumerate(scalars(ref, base + BODY, 0, SLOTS)):
        r = (code >= 9).astype(jnp.int32)
        c = code - 9 * r
        rows = pl.ds(pl.multiple_of(row + r * TILE, TILE), TILE)
        cols = pl.ds(pl.multiple_of(c * TILE, TILE), TILE)
        dst[rows, cols] = ref[base + s * TILE : base + (s + 1) * TILE, :]


def where_am_i():
    i = lax.axis_index("loop")
    j = lax.axis_index("group")
    return i >> 2, (i >> 1) & 1, i & 1, j >> 1, j & 1


def multiply(dense_left, dense_right, j, units):
    dense_right[...] = jnp.zeros_like(dense_right)
    for ref, base, y, c in units:
        place(dense_right, ref, base, (y * 2 + c) * 256)
    return jnp.dot(
        dense_left[j, :, : 8 * TILE], dense_right[:, : 8 * TILE], preferred_element_type=F32
    )


def round_units(refs, y, c):
    pair, beside = refs
    return (
        (pair, 0, y, c),
        (pair, UNIT, y, 1 - c),
        (beside, 0, 1 - y, c),
        (beside, UNIT, 1 - y, 1 - c),
    )


def begin(*refs):
    own, rounds, left = refs[:2], refs[2:10], refs[10:12]
    dense_left, product, dense_right = refs[12:]
    z, y, c, x, h = where_am_i()
    dense_left[...] = jnp.zeros_like(dense_left)
    for k in range(8):
        xx = (x, x ^ 1, 3 - x, (3 - x) ^ 1)[k >> 1]
        place(dense_left.at[xx * 2 + (h ^ (k & 1))], left[k >> 2], (k & 3) * UNIT, 0)
    product[...] = multiply(dense_left, dense_right, z, round_units(own, y, c))
    sign = 1 - 2 * c
    for r in (1, 2):
        near, far = rounds[4 * r - 4 : 4 * r - 2], rounds[4 * r - 2 : 4 * r]
        product[...] += multiply(
            dense_left, dense_right, (z - sign * r) & 7, round_units(near, y, c)
        )
        product[...] += multiply(
            dense_left, dense_right, (z + sign * r) & 7, round_units(far, y, 1 - c)
        )


def proceed(*refs):
    near, far = refs[:2], refs[2:4]
    dense_left, before, product, dense_right = refs[4:]
    z, y, c, _, _ = where_am_i()
    sign = 1 - 2 * c
    product[...] = before[...] + multiply(
        dense_left, dense_right, (z - sign * 3) & 7, round_units(near, y, c)
    )
    product[...] += multiply(
        dense_left, dense_right, (z + sign * 3) & 7, round_units(far, y, 1 - c)
    )


def half(ref, y, c, dense_left, dense_half):
    z = where_am_i()[0]
    dense_half[...] = jnp.zeros_like(dense_half)
    place(dense_half, ref, 0, c * 256)
    place(dense_half, ref, UNIT, (1 - c) * 256)
    return jnp.dot(
        dense_left[(z + 4) & 7, :, pl.ds(pl.multiple_of(y * 512, 512), 512)],
        dense_half[:, : 8 * TILE],
        preferred_element_type=F32,
    )


def add_half(pair, dense_left, before, product, dense_half):
    _, y, c, _, _ = where_am_i()
    product[...] = before[...] + half(pair, y, c, dense_left, dense_half)


def finish(codes, beside, dense_left, before, squares, sums, dense_half, product, held, sem):
    _, y, c, _, _ = where_am_i()
    product[...] = before[...] + half(beside, 1 - y, c, dense_left, dense_half)
    column = lax.broadcasted_iota(jnp.int32, (8, TILE), 0)
    total = jnp.zeros((8, TILE), F32)
    copies = []
    for s, code in enumerate(scalars(codes, 0, 0, 8)):
        used = code < 16
        p = code & 15
        rows = pl.ds(pl.multiple_of((p >> 3) * TILE, TILE), TILE)
        cols = pl.ds(pl.multiple_of((p & 7) * TILE, TILE), TILE)
        tile = product[rows, cols]
        tile = jnp.where(used, tile * tile, 0.0)
        held[s] = tile
        copies.append(pltpu.make_async_copy(held.at[s], squares.at[s], sem.at[s]))
        copies[-1].start()
        part = jnp.sum(tile, axis=0, keepdims=True)
        total += jnp.where(column == (p & 7), part, 0.0)
    for k in range(32):
        sums[k] = total
    for copy in copies:
        copy.wait()


def rescale(codes, squares, sums, out, marks, inside, parts, done, sem_in, sem_out):
    ins = [pltpu.make_async_copy(sums, parts, sem_in.at[8])]
    ins.append(pltpu.make_async_copy(codes, marks, sem_in.at[9]))
    ins += [pltpu.make_async_copy(squares.at[s], inside.at[s], sem_in.at[s]) for s in range(8)]
    for copy in ins:
        copy.start()
    ins[1].wait()
    at = scalars(marks, 0, 0, 8)
    ins[0].wait()
    factor = 8192.0 / jnp.sum(parts[...], axis=0)
    column = lax.broadcasted_iota(jnp.int32, (8, TILE), 0)
    outs = []
    for s in range(8):
        pick = jnp.where(column == (at[s] & 7), factor, 0.0)
        pick = jnp.sum(pick, axis=0, keepdims=True)
        ins[2 + s].wait()
        done[s] = inside[s] * pick
        outs.append(pltpu.make_async_copy(done.at[s], out.at[s], sem_out.at[s]))
        outs[-1].start()
    for copy in outs:
        copy.wait()


WHOLE = pl.BlockSpec(memory_space=pltpu.VMEM)
AWAY = pl.BlockSpec(memory_space=pl.ANY)
DENSE_LEFT = jax.ShapeDtypeStruct((8, 256, WIDE), BF16)
PRODUCT = jax.ShapeDtypeStruct((256, 1024), F32)
DENSE_RIGHT = pltpu.VMEM((1024, WIDE), BF16)
DENSE_HALF = pltpu.VMEM((512, WIDE), BF16)
TILES = (8, TILE, TILE)


def cost(blocks):
    return pl.CostEstimate(
        flops=blocks * 2**20, bytes_accessed=blocks * 2**16, transcendentals=0
    )


def shards(tile_values, tile_coords, tile_counts, result_coords, result_counts):
    slot = jnp.arange(16, dtype=jnp.int32)
    at = jnp.pad(tile_coords[0, 0], (0, 12))
    code = jnp.where(slot < tile_counts[0, 0], at + (at >> 3), 8).astype(BF16)
    unit = jnp.concatenate(
        [tile_values.reshape(BODY, TILE), jnp.broadcast_to(code[:, None], (16, TILE))]
    )

    def along(perm, v):
        return lax.ppermute(v, "loop", perm)

    def across(perm, v):
        return lax.ppermute(v, "group", perm)

    beside, crossed = along(YLO, unit), along(DIAGONAL, unit)
    pair = along(CORE, unit)
    first = jnp.concatenate([unit, pair])
    beside, crossed, _ = lax.optimization_barrier((beside, crossed, first))
    second = jnp.concatenate([beside, crossed])
    later, beside_later, _ = lax.optimization_barrier((unit, result_coords, first))
    row = jnp.concatenate([later, across(YHI, later)])
    at = jnp.pad(beside_later[0, 0], (0, 8))
    code = jnp.where(slot < result_counts[0, 0], at, at + 16).astype(BF16)
    codes = jnp.broadcast_to(code[:, None], (16, TILE))

    def after(v, *others):
        return lax.optimization_barrier((v, *others))

    streams = [first, second]
    right = [streams]
    row = jnp.concatenate([row, across(XNEAR, row)])
    left = [row, across(XMIRROR, row)]
    for r in range(3):
        if r == 2:
            streams = [streams[0], after(streams[1], *right[-3])[0]]
        ahead = along(RING, streams[0])
        behind = after(streams[1], ahead)[0] if r == 0 else streams[1]
        streams = [ahead, along(RING, behind)]
        other = after(*streams)
        right += [streams, [along(CORE, v) for v in other]]
    streams = [streams[0], after(streams[1], *right[-3])[0]]
    last = [along(RING, v) for v in streams]

    limit = pltpu.CompilerParams(vmem_limit_bytes=24 * 2**20)
    dense_left, product = pl.pallas_call(
        begin,
        in_specs=[WHOLE] * 12,
        out_specs=[WHOLE] * 2,
        out_shape=[DENSE_LEFT, PRODUCT],
        scratch_shapes=[DENSE_RIGHT],
        compiler_params=limit,
        cost_estimate=cost(6),
    )(*sum(right[:5], []), *left)
    product = pl.pallas_call(
        add_half,
        in_specs=[WHOLE] * 3,
        out_specs=WHOLE,
        out_shape=PRODUCT,
        scratch_shapes=[DENSE_HALF],
        compiler_params=limit,
        cost_estimate=cost(1),
    )(last[0], dense_left, product)
    product = pl.pallas_call(
        proceed,
        in_specs=[WHOLE] * 6,
        out_specs=WHOLE,
        out_shape=PRODUCT,
        scratch_shapes=[DENSE_RIGHT],
        compiler_params=limit,
        cost_estimate=cost(2),
    )(*sum(right[5:], []), dense_left, product)
    squares, sums = pl.pallas_call(
        finish,
        in_specs=[WHOLE] * 4,
        out_specs=[AWAY, WHOLE],
        out_shape=[jax.ShapeDtypeStruct(TILES, F32), jax.ShapeDtypeStruct((32, 8, TILE), F32)],
        scratch_shapes=[
            DENSE_HALF,
            pltpu.VMEM((256, 1024), F32),
            pltpu.VMEM(TILES, F32),
            pltpu.SemaphoreType.DMA((8,)),
        ],
        compiler_params=limit,
        cost_estimate=cost(1),
    )(codes, last[1], dense_left, product)
    sums = lax.all_to_all(sums, "loop", 0, 0, tiled=True)
    out = pl.pallas_call(
        rescale,
        in_specs=[AWAY] * 3,
        out_specs=AWAY,
        out_shape=jax.ShapeDtypeStruct(TILES, F32),
        scratch_shapes=[
            pltpu.VMEM((16, TILE), BF16),
            pltpu.VMEM(TILES, F32),
            pltpu.VMEM((32, 8, TILE), F32),
            pltpu.VMEM(TILES, F32),
            pltpu.SemaphoreType.DMA((10,)),
            pltpu.SemaphoreType.DMA((8,)),
        ],
        compiler_params=limit,
    )(codes, squares, sums)
    return out[None, None]


def solution(mesh):
    placed = (
        P("loop", "group", None, None, None),
        P("loop", "group", None),
        P("loop", "group"),
        P("loop", "group", None),
        P("loop", "group"),
    )
    return jax.shard_map(
        shards,
        mesh=mesh,
        in_specs=placed,
        out_specs=P("loop", "group", None, None, None),
        check_vma=False,
    )
```

```python
import jax
import jax.numpy as jnp
from jax import lax
from jax.experimental import pallas as pl
from jax.experimental.pallas import tpu as pltpu
from jax.sharding import PartitionSpec as P

TILE = 128
SLOTS = 4
BODY = SLOTS * TILE
UNIT = BODY + 16
WIDE = 9 * TILE
F32, BF16 = jnp.float32, jnp.bfloat16


def loop_perm(f):
    pairs = []
    for i in range(32):
        z, y, c = f(i >> 2, (i >> 1) & 1, i & 1)
        pairs.append((i, (z % 8) * 4 + y * 2 + c))
    return pairs


def group_perm(f):
    pairs = []
    for i in range(8):
        x, y = f(i >> 1, i & 1)
        pairs.append((i, (x % 4) * 2 + y))
    return pairs


CORE = loop_perm(lambda z, y, c: (z, y, 1 - c))
YLO = loop_perm(lambda z, y, c: (z, 1 - y, c))
DIAGONAL = loop_perm(lambda z, y, c: (z, 1 - y, 1 - c))
RING = loop_perm(lambda z, y, c: (z + 1 - 2 * c, y, c))
YHI = group_perm(lambda x, y: (x, 1 - y))
XNEAR = group_perm(lambda x, y: (x ^ 1, y))
XMIRROR = group_perm(lambda x, y: (3 - x, y))


def scalars(ref, base, first, count):
    marks = ref[base : base + 16, :].astype(F32)
    return [jnp.max(marks[s : s + 1, :]).astype(jnp.int32) for s in range(first, first + count)]


def place(dst, ref, base, row):
    for s, code in enumerate(scalars(ref, base + BODY, 0, SLOTS)):
        r = (code >= 9).astype(jnp.int32)
        c = code - 9 * r
        rows = pl.ds(pl.multiple_of(row + r * TILE, TILE), TILE)
        cols = pl.ds(pl.multiple_of(c * TILE, TILE), TILE)
        dst[rows, cols] = ref[base + s * TILE : base + (s + 1) * TILE, :]


def where_am_i():
    i = lax.axis_index("loop")
    j = lax.axis_index("group")
    return i >> 2, (i >> 1) & 1, i & 1, j >> 1, j & 1


def multiply(dense_left, dense_right, j, units):
    dense_right[...] = jnp.zeros_like(dense_right)
    for ref, base, y, c in units:
        place(dense_right, ref, base, (y * 2 + c) * 256)
    return jnp.dot(
        dense_left[j, :, : 8 * TILE], dense_right[:, : 8 * TILE], preferred_element_type=F32
    )


def round_units(refs, y, c):
    pair, beside = refs
    return (
        (pair, 0, y, c),
        (pair, UNIT, y, 1 - c),
        (beside, 0, 1 - y, c),
        (beside, UNIT, 1 - y, 1 - c),
    )


def begin(*refs):
    own, rounds, left = refs[:2], refs[2:10], refs[10:12]
    dense_left, product, dense_right = refs[12:]
    z, y, c, x, h = where_am_i()
    dense_left[...] = jnp.zeros_like(dense_left)
    for k in range(8):
        xx = (x, x ^ 1, 3 - x, (3 - x) ^ 1)[k >> 1]
        place(dense_left.at[xx * 2 + (h ^ (k & 1))], left[k >> 2], (k & 3) * UNIT, 0)
    product[...] = multiply(dense_left, dense_right, z, round_units(own, y, c))
    sign = 1 - 2 * c
    for r in (1, 2):
        near, far = rounds[4 * r - 4 : 4 * r - 2], rounds[4 * r - 2 : 4 * r]
        product[...] += multiply(
            dense_left, dense_right, (z - sign * r) & 7, round_units(near, y, c)
        )
        product[...] += multiply(
            dense_left, dense_right, (z + sign * r) & 7, round_units(far, y, 1 - c)
        )


def proceed(*refs):
    near, far = refs[:2], refs[2:4]
    dense_left, before, product, dense_right = refs[4:]
    z, y, c, _, _ = where_am_i()
    sign = 1 - 2 * c
    product[...] = before[...] + multiply(
        dense_left, dense_right, (z - sign * 3) & 7, round_units(near, y, c)
    )
    product[...] += multiply(
        dense_left, dense_right, (z + sign * 3) & 7, round_units(far, y, 1 - c)
    )


def half(ref, y, c, dense_left, dense_half):
    z = where_am_i()[0]
    dense_half[...] = jnp.zeros_like(dense_half)
    place(dense_half, ref, 0, c * 256)
    place(dense_half, ref, UNIT, (1 - c) * 256)
    return jnp.dot(
        dense_left[(z + 4) & 7, :, pl.ds(pl.multiple_of(y * 512, 512), 512)],
        dense_half[:, : 8 * TILE],
        preferred_element_type=F32,
    )


def add_half(pair, dense_left, before, product, dense_half):
    _, y, c, _, _ = where_am_i()
    product[...] = before[...] + half(pair, y, c, dense_left, dense_half)


def finish(codes, beside, dense_left, before, squares, sums, dense_half, product, held, sem):
    _, y, c, _, _ = where_am_i()
    product[...] = before[...] + half(beside, 1 - y, c, dense_left, dense_half)
    column = lax.broadcasted_iota(jnp.int32, (8, TILE), 0)
    total = jnp.zeros((8, TILE), F32)
    copies = []
    for s, code in enumerate(scalars(codes, 0, 0, 8)):
        used = code < 16
        p = code & 15
        rows = pl.ds(pl.multiple_of((p >> 3) * TILE, TILE), TILE)
        cols = pl.ds(pl.multiple_of((p & 7) * TILE, TILE), TILE)
        tile = product[rows, cols]
        tile = jnp.where(used, tile * tile, 0.0)
        held[s] = tile
        copies.append(pltpu.make_async_copy(held.at[s], squares.at[s], sem.at[s]))
        copies[-1].start()
        part = jnp.sum(tile, axis=0, keepdims=True)
        total += jnp.where(column == (p & 7), part, 0.0)
    for k in range(32):
        sums[k] = total
    for copy in copies:
        copy.wait()


def rescale(codes, squares, sums, out, marks, inside, parts, done, sem_in, sem_out):
    ins = [pltpu.make_async_copy(sums, parts, sem_in.at[8])]
    ins.append(pltpu.make_async_copy(codes, marks, sem_in.at[9]))
    ins += [pltpu.make_async_copy(squares.at[s], inside.at[s], sem_in.at[s]) for s in range(8)]
    for copy in ins:
        copy.start()
    ins[1].wait()
    at = scalars(marks, 0, 0, 8)
    ins[0].wait()
    factor = 8192.0 / jnp.sum(parts[...], axis=0)
    column = lax.broadcasted_iota(jnp.int32, (8, TILE), 0)
    outs = []
    for s in range(8):
        pick = jnp.where(column == (at[s] & 7), factor, 0.0)
        pick = jnp.sum(pick, axis=0, keepdims=True)
        ins[2 + s].wait()
        done[s] = inside[s] * pick
        outs.append(pltpu.make_async_copy(done.at[s], out.at[s], sem_out.at[s]))
        outs[-1].start()
    for copy in outs:
        copy.wait()


WHOLE = pl.BlockSpec(memory_space=pltpu.VMEM)
AWAY = pl.BlockSpec(memory_space=pl.ANY)
DENSE_LEFT = jax.ShapeDtypeStruct((8, 256, WIDE), BF16)
PRODUCT = jax.ShapeDtypeStruct((256, 1024), F32)
DENSE_RIGHT = pltpu.VMEM((1024, WIDE), BF16)
DENSE_HALF = pltpu.VMEM((512, WIDE), BF16)
TILES = (8, TILE, TILE)


def cost(blocks):
    return pl.CostEstimate(
        flops=blocks * 2 * 256 * 1024 * 1024, bytes_accessed=blocks * 4 * 2**20, transcendentals=0
    )


def shards(tile_values, tile_coords, tile_counts, result_coords, result_counts):
    slot = jnp.arange(16, dtype=jnp.int32)
    at = jnp.pad(tile_coords[0, 0], (0, 12))
    code = jnp.where(slot < tile_counts[0, 0], at + (at >> 3), 8).astype(BF16)
    unit = jnp.concatenate(
        [tile_values.reshape(BODY, TILE), jnp.broadcast_to(code[:, None], (16, TILE))]
    )

    def along(perm, v):
        return lax.ppermute(v, "loop", perm)

    def across(perm, v):
        return lax.ppermute(v, "group", perm)

    beside, crossed = along(YLO, unit), along(DIAGONAL, unit)
    pair = along(CORE, unit)
    first = jnp.concatenate([unit, pair])
    beside, crossed, _ = lax.optimization_barrier((beside, crossed, first))
    second = jnp.concatenate([beside, crossed])
    later, beside_later, _ = lax.optimization_barrier((unit, result_coords, first))
    row = jnp.concatenate([later, across(YHI, later)])
    at = jnp.pad(beside_later[0, 0], (0, 8))
    code = jnp.where(slot < result_counts[0, 0], at, at + 16).astype(BF16)
    codes = jnp.broadcast_to(code[:, None], (16, TILE))

    def after(v, *others):
        return lax.optimization_barrier((v, *others))

    streams = [first, second]
    right = [streams]
    row = jnp.concatenate([row, across(XNEAR, row)])
    left = [row, across(XMIRROR, row)]
    for r in range(3):
        ahead = along(RING, streams[0])
        behind = after(streams[1], ahead)[0] if r == 0 else streams[1]
        streams = [ahead, along(RING, behind)]
        other = streams
        right += [streams, [along(CORE, v) for v in other]]
    last = [along(RING, v) for v in streams]

    limit = pltpu.CompilerParams(vmem_limit_bytes=24 * 2**20)
    dense_left, product = pl.pallas_call(
        begin,
        in_specs=[WHOLE] * 12,
        out_specs=[WHOLE] * 2,
        out_shape=[DENSE_LEFT, PRODUCT],
        scratch_shapes=[DENSE_RIGHT],
        compiler_params=limit,
        cost_estimate=cost(6),
    )(*sum(right[:5], []), *left)
    product = pl.pallas_call(
        add_half,
        in_specs=[WHOLE] * 3,
        out_specs=WHOLE,
        out_shape=PRODUCT,
        scratch_shapes=[DENSE_HALF],
        compiler_params=limit,
        cost_estimate=cost(1),
    )(last[0], dense_left, product)
    product = pl.pallas_call(
        proceed,
        in_specs=[WHOLE] * 6,
        out_specs=WHOLE,
        out_shape=PRODUCT,
        scratch_shapes=[DENSE_RIGHT],
        compiler_params=limit,
        cost_estimate=cost(2),
    )(*sum(right[5:], []), dense_left, product)
    squares, sums = pl.pallas_call(
        finish,
        in_specs=[WHOLE] * 4,
        out_specs=[AWAY, WHOLE],
        out_shape=[jax.ShapeDtypeStruct(TILES, F32), jax.ShapeDtypeStruct((32, 8, TILE), F32)],
        scratch_shapes=[
            DENSE_HALF,
            pltpu.VMEM((256, 1024), F32),
            pltpu.VMEM(TILES, F32),
            pltpu.SemaphoreType.DMA((8,)),
        ],
        compiler_params=limit,
        cost_estimate=cost(1),
    )(codes, last[1], dense_left, product)
    sums = lax.all_to_all(sums, "loop", 0, 0, tiled=True)
    out = pl.pallas_call(
        rescale,
        in_specs=[AWAY] * 3,
        out_specs=AWAY,
        out_shape=jax.ShapeDtypeStruct(TILES, F32),
        scratch_shapes=[
            pltpu.VMEM((16, TILE), BF16),
            pltpu.VMEM(TILES, F32),
            pltpu.VMEM((32, 8, TILE), F32),
            pltpu.VMEM(TILES, F32),
            pltpu.SemaphoreType.DMA((10,)),
            pltpu.SemaphoreType.DMA((8,)),
        ],
        compiler_params=limit,
    )(codes, squares, sums)
    return out[None, None]


def solution(mesh):
    placed = (
        P("loop", "group", None, None, None),
        P("loop", "group", None),
        P("loop", "group"),
        P("loop", "group", None),
        P("loop", "group"),
    )
    return jax.shard_map(
        shards,
        mesh=mesh,
        in_specs=placed,
        out_specs=P("loop", "group", None, None, None),
        check_vma=False,
    )
```

```python
import jax
import jax.numpy as jnp
from jax import lax
from jax.experimental import pallas as pl
from jax.experimental.pallas import tpu as pltpu
from jax.sharding import PartitionSpec as P

TILE = 128
SLOTS = 4
BODY = SLOTS * TILE
UNIT = BODY + 16
WIDE = 9 * TILE
F32, BF16 = jnp.float32, jnp.bfloat16


def loop_perm(f):
    pairs = []
    for i in range(32):
        z, y, c = f(i >> 2, (i >> 1) & 1, i & 1)
        pairs.append((i, (z % 8) * 4 + y * 2 + c))
    return pairs


def group_perm(f):
    pairs = []
    for i in range(8):
        x, y = f(i >> 1, i & 1)
        pairs.append((i, (x % 4) * 2 + y))
    return pairs


CORE = loop_perm(lambda z, y, c: (z, y, 1 - c))
YLO = loop_perm(lambda z, y, c: (z, 1 - y, c))
DIAGONAL = loop_perm(lambda z, y, c: (z, 1 - y, 1 - c))
RING = loop_perm(lambda z, y, c: (z + 1 - 2 * c, y, c))
YHI = group_perm(lambda x, y: (x, 1 - y))
XNEAR = group_perm(lambda x, y: (x ^ 1, y))
XMIRROR = group_perm(lambda x, y: (3 - x, y))


def scalars(ref, base, first, count):
    marks = ref[base : base + 16, :].astype(F32)
    return [jnp.max(marks[s : s + 1, :]).astype(jnp.int32) for s in range(first, first + count)]


def place(dst, ref, base, row):
    for s, code in enumerate(scalars(ref, base + BODY, 0, SLOTS)):
        r = (code >= 9).astype(jnp.int32)
        c = code - 9 * r
        rows = pl.ds(pl.multiple_of(row + r * TILE, TILE), TILE)
        cols = pl.ds(pl.multiple_of(c * TILE, TILE), TILE)
        dst[rows, cols] = ref[base + s * TILE : base + (s + 1) * TILE, :]


def where_am_i():
    i = lax.axis_index("loop")
    j = lax.axis_index("group")
    return i >> 2, (i >> 1) & 1, i & 1, j >> 1, j & 1


def multiply(dense_left, jobs, buffers):
    for k, (j, units) in enumerate(jobs):
        dense_right = buffers[k % len(buffers)]
        dense_right[...] = jnp.zeros_like(dense_right)
        for ref, base, y, c in units:
            place(dense_right, ref, base, (y * 2 + c) * 256)
        yield jnp.dot(
            dense_left[j, :, : 8 * TILE], dense_right[:, : 8 * TILE], preferred_element_type=F32
        )


def round_units(refs, y, c):
    pair, beside = refs
    return (
        (pair, 0, y, c),
        (pair, UNIT, y, 1 - c),
        (beside, 0, 1 - y, c),
        (beside, UNIT, 1 - y, 1 - c),
    )


def begin(*refs):
    own, rounds, left = refs[:2], refs[2:10], refs[10:12]
    dense_left, product, *dense_right = refs[12:]
    z, y, c, x, h = where_am_i()
    dense_left[...] = jnp.zeros_like(dense_left)
    for k in range(8):
        xx = (x, x ^ 1, 3 - x, (3 - x) ^ 1)[k >> 1]
        place(dense_left.at[xx * 2 + (h ^ (k & 1))], left[k >> 2], (k & 3) * UNIT, 0)
    sign = 1 - 2 * c
    jobs = [(z, round_units(own, y, c))]
    for r in (1, 2):
        near, far = rounds[4 * r - 4 : 4 * r - 2], rounds[4 * r - 2 : 4 * r]
        jobs.append(((z - sign * r) & 7, round_units(near, y, c)))
        jobs.append(((z + sign * r) & 7, round_units(far, y, 1 - c)))
    for k, part in enumerate(multiply(dense_left, jobs, dense_right)):
        product[...] = part if k == 0 else product[...] + part


def proceed(*refs):
    near, far = refs[:2], refs[2:4]
    dense_left, before, product, *dense_right = refs[4:]
    z, y, c, _, _ = where_am_i()
    sign = 1 - 2 * c
    jobs = [
        ((z - sign * 3) & 7, round_units(near, y, c)),
        ((z + sign * 3) & 7, round_units(far, y, 1 - c)),
    ]
    for k, part in enumerate(multiply(dense_left, jobs, dense_right)):
        product[...] = (before if k == 0 else product)[...] + part


def half(ref, y, c, dense_left, dense_half):
    z = where_am_i()[0]
    dense_half[...] = jnp.zeros_like(dense_half)
    place(dense_half, ref, 0, c * 256)
    place(dense_half, ref, UNIT, (1 - c) * 256)
    return jnp.dot(
        dense_left[(z + 4) & 7, :, pl.ds(pl.multiple_of(y * 512, 512), 512)],
        dense_half[:, : 8 * TILE],
        preferred_element_type=F32,
    )


def add_half(pair, dense_left, before, product, dense_half):
    _, y, c, _, _ = where_am_i()
    product[...] = before[...] + half(pair, y, c, dense_left, dense_half)


def finish(codes, beside, dense_left, before, squares, sums, dense_half, product, held, sem):
    _, y, c, _, _ = where_am_i()
    product[...] = before[...] + half(beside, 1 - y, c, dense_left, dense_half)
    column = lax.broadcasted_iota(jnp.int32, (8, TILE), 0)
    total = jnp.zeros((8, TILE), F32)
    copies = []
    for s, code in enumerate(scalars(codes, 0, 0, 8)):
        used = code < 16
        p = code & 15
        rows = pl.ds(pl.multiple_of((p >> 3) * TILE, TILE), TILE)
        cols = pl.ds(pl.multiple_of((p & 7) * TILE, TILE), TILE)
        tile = product[rows, cols]
        tile = jnp.where(used, tile * tile, 0.0)
        held[s] = tile
        copies.append(pltpu.make_async_copy(held.at[s], squares.at[s], sem.at[s]))
        copies[-1].start()
        part = jnp.sum(tile, axis=0, keepdims=True)
        total += jnp.where(column == (p & 7), part, 0.0)
    for k in range(32):
        sums[k] = total
    for copy in copies:
        copy.wait()


def rescale(codes, squares, sums, out, marks, inside, parts, done, sem_in, sem_out):
    ins = [pltpu.make_async_copy(sums, parts, sem_in.at[8])]
    ins.append(pltpu.make_async_copy(codes, marks, sem_in.at[9]))
    ins += [pltpu.make_async_copy(squares.at[s], inside.at[s], sem_in.at[s]) for s in range(8)]
    for copy in ins:
        copy.start()
    ins[1].wait()
    at = scalars(marks, 0, 0, 8)
    ins[0].wait()
    factor = 8192.0 / jnp.sum(parts[...], axis=0)
    column = lax.broadcasted_iota(jnp.int32, (8, TILE), 0)
    outs = []
    for s in range(8):
        pick = jnp.where(column == (at[s] & 7), factor, 0.0)
        pick = jnp.sum(pick, axis=0, keepdims=True)
        ins[2 + s].wait()
        done[s] = inside[s] * pick
        outs.append(pltpu.make_async_copy(done.at[s], out.at[s], sem_out.at[s]))
        outs[-1].start()
    for copy in outs:
        copy.wait()


WHOLE = pl.BlockSpec(memory_space=pltpu.VMEM)
AWAY = pl.BlockSpec(memory_space=pl.ANY)
DENSE_LEFT = jax.ShapeDtypeStruct((8, 256, WIDE), BF16)
PRODUCT = jax.ShapeDtypeStruct((256, 1024), F32)
DENSE_RIGHT = pltpu.VMEM((1024, WIDE), BF16)
DENSE_HALF = pltpu.VMEM((512, WIDE), BF16)
TILES = (8, TILE, TILE)


def cost(blocks):
    return pl.CostEstimate(
        flops=blocks * 2 * 256 * 1024 * 1024, bytes_accessed=blocks * 4 * 2**20, transcendentals=0
    )


def shards(tile_values, tile_coords, tile_counts, result_coords, result_counts):
    slot = jnp.arange(16, dtype=jnp.int32)
    at = jnp.pad(tile_coords[0, 0], (0, 12))
    code = jnp.where(slot < tile_counts[0, 0], at + (at >> 3), 8).astype(BF16)
    unit = jnp.concatenate(
        [tile_values.reshape(BODY, TILE), jnp.broadcast_to(code[:, None], (16, TILE))]
    )

    def along(perm, v):
        return lax.ppermute(v, "loop", perm)

    def across(perm, v):
        return lax.ppermute(v, "group", perm)

    beside, crossed = along(YLO, unit), along(DIAGONAL, unit)
    pair = along(CORE, unit)
    first = jnp.concatenate([unit, pair])
    beside, crossed, _ = lax.optimization_barrier((beside, crossed, first))
    second = jnp.concatenate([beside, crossed])
    later, beside_later, _ = lax.optimization_barrier((unit, result_coords, first))
    row = jnp.concatenate([later, across(YHI, later)])
    at = jnp.pad(beside_later[0, 0], (0, 8))
    code = jnp.where(slot < result_counts[0, 0], at, at + 16).astype(BF16)
    codes = jnp.broadcast_to(code[:, None], (16, TILE))

    def after(v, *others):
        return lax.optimization_barrier((v, *others))

    streams = [first, second]
    right = [streams]
    row = jnp.concatenate([row, across(XNEAR, row)])
    left = [row, across(XMIRROR, row)]
    for r in range(3):
        ahead = along(RING, streams[0])
        behind = after(streams[1], ahead)[0] if r == 0 else streams[1]
        streams = [ahead, along(RING, behind)]
        other = streams
        right += [streams, [along(CORE, v) for v in other]]
    last = [along(RING, v) for v in streams]

    limit = pltpu.CompilerParams(vmem_limit_bytes=24 * 2**20)
    dense_left, product = pl.pallas_call(
        begin,
        in_specs=[WHOLE] * 12,
        out_specs=[WHOLE] * 2,
        out_shape=[DENSE_LEFT, PRODUCT],
        scratch_shapes=[DENSE_RIGHT] * 2,
        compiler_params=limit,
        cost_estimate=cost(6),
    )(*sum(right[:5], []), *left)
    product = pl.pallas_call(
        add_half,
        in_specs=[WHOLE] * 3,
        out_specs=WHOLE,
        out_shape=PRODUCT,
        scratch_shapes=[DENSE_HALF],
        compiler_params=limit,
        cost_estimate=cost(1),
    )(last[0], dense_left, product)
    product = pl.pallas_call(
        proceed,
        in_specs=[WHOLE] * 6,
        out_specs=WHOLE,
        out_shape=PRODUCT,
        scratch_shapes=[DENSE_RIGHT] * 2,
        compiler_params=limit,
        cost_estimate=cost(2),
    )(*sum(right[5:], []), dense_left, product)
    squares, sums = pl.pallas_call(
        finish,
        in_specs=[WHOLE] * 4,
        out_specs=[AWAY, WHOLE],
        out_shape=[jax.ShapeDtypeStruct(TILES, F32), jax.ShapeDtypeStruct((32, 8, TILE), F32)],
        scratch_shapes=[
            DENSE_HALF,
            pltpu.VMEM((256, 1024), F32),
            pltpu.VMEM(TILES, F32),
            pltpu.SemaphoreType.DMA((8,)),
        ],
        compiler_params=limit,
        cost_estimate=cost(1),
    )(codes, last[1], dense_left, product)
    sums = lax.all_to_all(sums, "loop", 0, 0, tiled=True)
    out = pl.pallas_call(
        rescale,
        in_specs=[AWAY] * 3,
        out_specs=AWAY,
        out_shape=jax.ShapeDtypeStruct(TILES, F32),
        scratch_shapes=[
            pltpu.VMEM((16, TILE), BF16),
            pltpu.VMEM(TILES, F32),
            pltpu.VMEM((32, 8, TILE), F32),
            pltpu.VMEM(TILES, F32),
            pltpu.SemaphoreType.DMA((10,)),
            pltpu.SemaphoreType.DMA((8,)),
        ],
        compiler_params=limit,
    )(codes, squares, sums)
    return out[None, None]


def solution(mesh):
    placed = (
        P("loop", "group", None, None, None),
        P("loop", "group", None),
        P("loop", "group"),
        P("loop", "group", None),
        P("loop", "group"),
    )
    return jax.shard_map(
        shards,
        mesh=mesh,
        in_specs=placed,
        out_specs=P("loop", "group", None, None, None),
        check_vma=False,
    )
```

```python
import jax
import jax.numpy as jnp
from jax import lax
from jax.experimental import pallas as pl
from jax.experimental.pallas import tpu as pltpu
from jax.sharding import PartitionSpec as P

TILE = 128
SLOTS = 4
BODY = SLOTS * TILE
UNIT = BODY + 16
WIDE = 9 * TILE
F32, BF16 = jnp.float32, jnp.bfloat16


def loop_perm(f):
    pairs = []
    for i in range(32):
        z, y, c = f(i >> 2, (i >> 1) & 1, i & 1)
        pairs.append((i, (z % 8) * 4 + y * 2 + c))
    return pairs


def group_perm(f):
    pairs = []
    for i in range(8):
        x, y = f(i >> 1, i & 1)
        pairs.append((i, (x % 4) * 2 + y))
    return pairs


CORE = loop_perm(lambda z, y, c: (z, y, 1 - c))
YLO = loop_perm(lambda z, y, c: (z, 1 - y, c))
DIAGONAL = loop_perm(lambda z, y, c: (z, 1 - y, 1 - c))
RING = loop_perm(lambda z, y, c: (z + 1 - 2 * c, y, c))
YHI = group_perm(lambda x, y: (x, 1 - y))
XNEAR = group_perm(lambda x, y: (x ^ 1, y))
XMIRROR = group_perm(lambda x, y: (3 - x, y))


def scalars(ref, base, first, count):
    marks = ref[base : base + 16, :].astype(F32)
    return [jnp.max(marks[s : s + 1, :]).astype(jnp.int32) for s in range(first, first + count)]


def place(dst, ref, base, row):
    for s, code in enumerate(scalars(ref, base + BODY, 0, SLOTS)):
        r = (code >= 9).astype(jnp.int32)
        c = code - 9 * r
        rows = pl.ds(pl.multiple_of(row + r * TILE, TILE), TILE)
        cols = pl.ds(pl.multiple_of(c * TILE, TILE), TILE)
        dst[rows, cols] = ref[base + s * TILE : base + (s + 1) * TILE, :]


def where_am_i():
    i = lax.axis_index("loop")
    j = lax.axis_index("group")
    return i >> 2, (i >> 1) & 1, i & 1, j >> 1, j & 1


def multiply(dense_left, jobs, buffers):
    for k, (j, units) in enumerate(jobs):
        dense_right = buffers[k % len(buffers)]
        dense_right[...] = jnp.zeros_like(dense_right)
        for ref, base, y, c in units:
            place(dense_right, ref, base, (y * 2 + c) * 256)
        yield jnp.dot(
            dense_left[j, :, : 8 * TILE], dense_right[:, : 8 * TILE], preferred_element_type=F32
        )


def round_units(refs, y, c):
    pair, beside = refs
    return (
        (pair, 0, y, c),
        (pair, UNIT, y, 1 - c),
        (beside, 0, 1 - y, c),
        (beside, UNIT, 1 - y, 1 - c),
    )


def begin(*refs):
    own, rounds, left = refs[:2], refs[2:10], refs[10:12]
    dense_left, product, *dense_right = refs[12:]
    z, y, c, x, h = where_am_i()
    dense_left[...] = jnp.zeros_like(dense_left)
    for k in range(8):
        xx = (x, x ^ 1, 3 - x, (3 - x) ^ 1)[k >> 1]
        place(dense_left.at[xx * 2 + (h ^ (k & 1))], left[k >> 2], (k & 3) * UNIT, 0)
    sign = 1 - 2 * c
    jobs = [(z, round_units(own, y, c))]
    for r in (1, 2):
        near, far = rounds[4 * r - 4 : 4 * r - 2], rounds[4 * r - 2 : 4 * r]
        jobs.append(((z - sign * r) & 7, round_units(near, y, c)))
        jobs.append(((z + sign * r) & 7, round_units(far, y, 1 - c)))
    for k, part in enumerate(multiply(dense_left, jobs, dense_right)):
        product[...] = part if k == 0 else product[...] + part


def proceed(*refs):
    near, far = refs[:2], refs[2:4]
    dense_left, before, product, *dense_right = refs[4:]
    z, y, c, _, _ = where_am_i()
    sign = 1 - 2 * c
    jobs = [
        ((z - sign * 3) & 7, round_units(near, y, c)),
        ((z + sign * 3) & 7, round_units(far, y, 1 - c)),
    ]
    for k, part in enumerate(multiply(dense_left, jobs, dense_right)):
        product[...] = (before if k == 0 else product)[...] + part


def half(ref, y, c, dense_left, dense_half):
    z = where_am_i()[0]
    dense_half[...] = jnp.zeros_like(dense_half)
    place(dense_half, ref, 0, c * 256)
    place(dense_half, ref, UNIT, (1 - c) * 256)
    return jnp.dot(
        dense_left[(z + 4) & 7, :, pl.ds(pl.multiple_of(y * 512, 512), 512)],
        dense_half[:, : 8 * TILE],
        preferred_element_type=F32,
    )


def add_half(pair, dense_left, before, product, dense_half):
    _, y, c, _, _ = where_am_i()
    product[...] = before[...] + half(pair, y, c, dense_left, dense_half)


def finish(codes, beside, dense_left, before, squares, sums, dense_half, product, held, sem):
    _, y, c, _, _ = where_am_i()
    product[...] = before[...] + half(beside, 1 - y, c, dense_left, dense_half)
    column = lax.broadcasted_iota(jnp.int32, (8, TILE), 0)
    total = jnp.zeros((8, TILE), F32)
    copies = []
    for s, code in enumerate(scalars(codes, 0, 0, 8)):
        used = code < 16
        p = code & 15
        rows = pl.ds(pl.multiple_of((p >> 3) * TILE, TILE), TILE)
        cols = pl.ds(pl.multiple_of((p & 7) * TILE, TILE), TILE)
        tile = product[rows, cols]
        tile = jnp.where(used, tile * tile, 0.0)
        held[s] = tile
        copies.append(pltpu.make_async_copy(held.at[s], squares.at[s], sem.at[s]))
        copies[-1].start()
        part = jnp.sum(tile, axis=0, keepdims=True)
        total += jnp.where(column == (p & 7), part, 0.0)
    for k in range(32):
        sums[k] = total
    for copy in copies:
        copy.wait()


def rescale(codes, squares, sums, out, marks, inside, parts, done, sem_in, sem_out):
    ins = [pltpu.make_async_copy(sums, parts, sem_in.at[8])]
    ins.append(pltpu.make_async_copy(codes, marks, sem_in.at[9]))
    ins += [pltpu.make_async_copy(squares.at[s], inside.at[s], sem_in.at[s]) for s in range(8)]
    for copy in ins:
        copy.start()
    ins[1].wait()
    at = scalars(marks, 0, 0, 8)
    ins[0].wait()
    factor = 8192.0 / jnp.sum(parts[...], axis=0)
    column = lax.broadcasted_iota(jnp.int32, (8, TILE), 0)
    outs = []
    for s in range(8):
        pick = jnp.where(column == (at[s] & 7), factor, 0.0)
        pick = jnp.sum(pick, axis=0, keepdims=True)
        ins[2 + s].wait()
        done[s] = inside[s] * pick
        outs.append(pltpu.make_async_copy(done.at[s], out.at[s], sem_out.at[s]))
        outs[-1].start()
    for copy in outs:
        copy.wait()


WHOLE = pl.BlockSpec(memory_space=pltpu.VMEM)
AWAY = pl.BlockSpec(memory_space=pl.ANY)
DENSE_LEFT = jax.ShapeDtypeStruct((8, 256, WIDE), BF16)
PRODUCT = jax.ShapeDtypeStruct((256, 1024), F32)
DENSE_RIGHT = pltpu.VMEM((1024, WIDE), BF16)
DENSE_HALF = pltpu.VMEM((512, WIDE), BF16)
TILES = (8, TILE, TILE)


def cost(blocks):
    return pl.CostEstimate(
        flops=blocks * 2 * 256 * 1024 * 1024, bytes_accessed=blocks * 4 * 2**20, transcendentals=0
    )


def shards(tile_values, tile_coords, tile_counts, result_coords, result_counts):
    slot = jnp.arange(16, dtype=jnp.int32)
    at = jnp.pad(tile_coords[0, 0], (0, 12))
    code = jnp.where(slot < tile_counts[0, 0], at + (at >> 3), 8).astype(BF16)
    unit = jnp.concatenate(
        [tile_values.reshape(BODY, TILE), jnp.broadcast_to(code[:, None], (16, TILE))]
    )

    unit = lax.optimization_barrier(unit)

    def along(perm, v):
        return lax.ppermute(v, "loop", perm)

    def across(perm, v):
        return lax.ppermute(v, "group", perm)

    beside, crossed = along(YLO, unit), along(DIAGONAL, unit)
    pair = along(CORE, unit)
    first = jnp.concatenate([unit, pair])
    beside, crossed, _ = lax.optimization_barrier((beside, crossed, first))
    second = jnp.concatenate([beside, crossed])
    later, beside_later, _ = lax.optimization_barrier((unit, result_coords, first))
    row = jnp.concatenate([later, across(YHI, later)])
    at = jnp.pad(beside_later[0, 0], (0, 8))
    code = jnp.where(slot < result_counts[0, 0], at, at + 16).astype(BF16)
    codes = jnp.broadcast_to(code[:, None], (16, TILE))

    def after(v, *others):
        return lax.optimization_barrier((v, *others))

    streams = [first, second]
    right = [streams]
    row = jnp.concatenate([row, across(XNEAR, row)])
    left = [row, across(XMIRROR, row)]
    for r in range(3):
        ahead = along(RING, streams[0])
        behind = after(streams[1], ahead)[0] if r == 0 else streams[1]
        streams = [ahead, along(RING, behind)]
        other = streams
        right += [streams, [along(CORE, v) for v in other]]
    last = [along(RING, v) for v in streams]

    limit = pltpu.CompilerParams(vmem_limit_bytes=24 * 2**20)
    dense_left, product = pl.pallas_call(
        begin,
        in_specs=[WHOLE] * 12,
        out_specs=[WHOLE] * 2,
        out_shape=[DENSE_LEFT, PRODUCT],
        scratch_shapes=[DENSE_RIGHT] * 2,
        compiler_params=limit,
        cost_estimate=cost(6),
    )(*sum(right[:5], []), *left)
    product = pl.pallas_call(
        add_half,
        in_specs=[WHOLE] * 3,
        out_specs=WHOLE,
        out_shape=PRODUCT,
        scratch_shapes=[DENSE_HALF],
        compiler_params=limit,
        cost_estimate=cost(1),
    )(last[0], dense_left, product)
    product = pl.pallas_call(
        proceed,
        in_specs=[WHOLE] * 6,
        out_specs=WHOLE,
        out_shape=PRODUCT,
        scratch_shapes=[DENSE_RIGHT] * 2,
        compiler_params=limit,
        cost_estimate=cost(2),
    )(*sum(right[5:], []), dense_left, product)
    squares, sums = pl.pallas_call(
        finish,
        in_specs=[WHOLE] * 4,
        out_specs=[AWAY, WHOLE],
        out_shape=[jax.ShapeDtypeStruct(TILES, F32), jax.ShapeDtypeStruct((32, 8, TILE), F32)],
        scratch_shapes=[
            DENSE_HALF,
            pltpu.VMEM((256, 1024), F32),
            pltpu.VMEM(TILES, F32),
            pltpu.SemaphoreType.DMA((8,)),
        ],
        compiler_params=limit,
        cost_estimate=cost(1),
    )(codes, last[1], dense_left, product)
    sums = lax.all_to_all(sums, "loop", 0, 0, tiled=True)
    out = pl.pallas_call(
        rescale,
        in_specs=[AWAY] * 3,
        out_specs=AWAY,
        out_shape=jax.ShapeDtypeStruct(TILES, F32),
        scratch_shapes=[
            pltpu.VMEM((16, TILE), BF16),
            pltpu.VMEM(TILES, F32),
            pltpu.VMEM((32, 8, TILE), F32),
            pltpu.VMEM(TILES, F32),
            pltpu.SemaphoreType.DMA((10,)),
            pltpu.SemaphoreType.DMA((8,)),
        ],
        compiler_params=limit,
    )(codes, squares, sums)
    return out[None, None]


def solution(mesh):
    placed = (
        P("loop", "group", None, None, None),
        P("loop", "group", None),
        P("loop", "group"),
        P("loop", "group", None),
        P("loop", "group"),
    )
    return jax.shard_map(
        shards,
        mesh=mesh,
        in_specs=placed,
        out_specs=P("loop", "group", None, None, None),
        check_vma=False,
    )
```

```python
import jax
import jax.numpy as jnp
from jax import lax
from jax.experimental import pallas as pl
from jax.experimental.pallas import tpu as pltpu
from jax.sharding import PartitionSpec as P

TILE = 128
SLOTS = 4
BODY = SLOTS * TILE
UNIT = BODY + 16
WIDE = 9 * TILE
F32, BF16 = jnp.float32, jnp.bfloat16


def loop_perm(f):
    pairs = []
    for i in range(32):
        z, y, c = f(i >> 2, (i >> 1) & 1, i & 1)
        pairs.append((i, (z % 8) * 4 + y * 2 + c))
    return pairs


def group_perm(f):
    pairs = []
    for i in range(8):
        x, y = f(i >> 1, i & 1)
        pairs.append((i, (x % 4) * 2 + y))
    return pairs


CORE = loop_perm(lambda z, y, c: (z, y, 1 - c))
YLO = loop_perm(lambda z, y, c: (z, 1 - y, c))
DIAGONAL = loop_perm(lambda z, y, c: (z, 1 - y, 1 - c))
RING = loop_perm(lambda z, y, c: (z + 1 - 2 * c, y, c))
YHI = group_perm(lambda x, y: (x, 1 - y))
XNEAR = group_perm(lambda x, y: (x ^ 1, y))
XMIRROR = group_perm(lambda x, y: (3 - x, y))


def scalars(ref, base, first, count):
    marks = ref[base : base + 16, :].astype(F32)
    return [jnp.max(marks[s : s + 1, :]).astype(jnp.int32) for s in range(first, first + count)]


def place(dst, ref, base, row):
    for s, code in enumerate(scalars(ref, base + BODY, 0, SLOTS)):
        r = (code >= 9).astype(jnp.int32)
        c = code - 9 * r
        rows = pl.ds(pl.multiple_of(row + r * TILE, TILE), TILE)
        cols = pl.ds(pl.multiple_of(c * TILE, TILE), TILE)
        dst[rows, cols] = ref[base + s * TILE : base + (s + 1) * TILE, :]


def where_am_i():
    i = lax.axis_index("loop")
    j = lax.axis_index("group")
    return i >> 2, (i >> 1) & 1, i & 1, j >> 1, j & 1


def multiply(dense_left, jobs, buffers):
    for k, (j, units) in enumerate(jobs):
        dense_right = buffers[k % len(buffers)]
        dense_right[...] = jnp.zeros_like(dense_right)
        for ref, base, y, c in units:
            place(dense_right, ref, base, (y * 2 + c) * 256)
        yield jnp.dot(
            dense_left[j, :, : 8 * TILE], dense_right[:, : 8 * TILE], preferred_element_type=F32
        )


def round_units(refs, y, c):
    pair, beside = refs
    return (
        (pair, 0, y, c),
        (pair, UNIT, y, 1 - c),
        (beside, 0, 1 - y, c),
        (beside, UNIT, 1 - y, 1 - c),
    )


def begin(*refs):
    own, rounds, left = refs[:2], refs[2:10], refs[10:12]
    dense_left, product, *dense_right = refs[12:]
    z, y, c, x, h = where_am_i()
    dense_left[...] = jnp.zeros_like(dense_left)
    for k in range(8):
        xx = (x, x ^ 1, 3 - x, (3 - x) ^ 1)[k >> 1]
        place(dense_left.at[xx * 2 + (h ^ (k & 1))], left[k >> 2], (k & 3) * UNIT, 0)
    sign = 1 - 2 * c
    jobs = [(z, round_units(own, y, c))]
    for r in (1, 2):
        near, far = rounds[4 * r - 4 : 4 * r - 2], rounds[4 * r - 2 : 4 * r]
        jobs.append(((z - sign * r) & 7, round_units(near, y, c)))
        jobs.append(((z + sign * r) & 7, round_units(far, y, 1 - c)))
    for k, part in enumerate(multiply(dense_left, jobs, dense_right)):
        product[...] = part if k == 0 else product[...] + part


def proceed(*refs):
    near, far = refs[:2], refs[2:4]
    dense_left, before, product, *dense_right = refs[4:]
    z, y, c, _, _ = where_am_i()
    sign = 1 - 2 * c
    jobs = [
        ((z - sign * 3) & 7, round_units(near, y, c)),
        ((z + sign * 3) & 7, round_units(far, y, 1 - c)),
    ]
    for k, part in enumerate(multiply(dense_left, jobs, dense_right)):
        product[...] = (before if k == 0 else product)[...] + part


def half(ref, y, c, dense_left, dense_half):
    z = where_am_i()[0]
    dense_half[...] = jnp.zeros_like(dense_half)
    place(dense_half, ref, 0, c * 256)
    place(dense_half, ref, UNIT, (1 - c) * 256)
    return jnp.dot(
        dense_left[(z + 4) & 7, :, pl.ds(pl.multiple_of(y * 512, 512), 512)],
        dense_half[:, : 8 * TILE],
        preferred_element_type=F32,
    )


def add_half(pair, dense_left, before, product, dense_half):
    _, y, c, _, _ = where_am_i()
    product[...] = before[...] + half(pair, y, c, dense_left, dense_half)


def finish(codes, beside, dense_left, before, squares, sums, dense_half, product, held, sem):
    _, y, c, _, _ = where_am_i()
    product[...] = before[...] + half(beside, 1 - y, c, dense_left, dense_half)
    column = lax.broadcasted_iota(jnp.int32, (8, TILE), 0)
    total = jnp.zeros((8, TILE), F32)
    copies = []
    for s, code in enumerate(scalars(codes, 0, 0, 8)):
        used = code < 16
        p = code & 15
        rows = pl.ds(pl.multiple_of((p >> 3) * TILE, TILE), TILE)
        cols = pl.ds(pl.multiple_of((p & 7) * TILE, TILE), TILE)
        tile = product[rows, cols]
        tile = jnp.where(used, tile * tile, 0.0)
        held[s] = tile
        copies.append(pltpu.make_async_copy(held.at[s], squares.at[s], sem.at[s]))
        copies[-1].start()
        part = jnp.sum(tile, axis=0, keepdims=True)
        total += jnp.where(column == (p & 7), part, 0.0)
    for k in range(32):
        sums[k] = total
    for copy in copies:
        copy.wait()


def rescale(codes, squares, sums, out, marks, inside, parts, done, sem_in, sem_out):
    ins = [pltpu.make_async_copy(sums, parts, sem_in.at[8])]
    ins.append(pltpu.make_async_copy(codes, marks, sem_in.at[9]))
    ins += [pltpu.make_async_copy(squares.at[s], inside.at[s], sem_in.at[s]) for s in range(8)]
    for copy in ins:
        copy.start()
    ins[1].wait()
    at = scalars(marks, 0, 0, 8)
    ins[0].wait()
    factor = 8192.0 / jnp.sum(parts[...], axis=0)
    column = lax.broadcasted_iota(jnp.int32, (8, TILE), 0)
    outs = []
    for s in range(8):
        pick = jnp.where(column == (at[s] & 7), factor, 0.0)
        pick = jnp.sum(pick, axis=0, keepdims=True)
        ins[2 + s].wait()
        done[s] = inside[s] * pick
        outs.append(pltpu.make_async_copy(done.at[s], out.at[s], sem_out.at[s]))
        outs[-1].start()
    for copy in outs:
        copy.wait()


WHOLE = pl.BlockSpec(memory_space=pltpu.VMEM)
AWAY = pl.BlockSpec(memory_space=pl.ANY)
DENSE_LEFT = jax.ShapeDtypeStruct((8, 256, WIDE), BF16)
PRODUCT = jax.ShapeDtypeStruct((256, 1024), F32)
DENSE_RIGHT = pltpu.VMEM((1024, WIDE), BF16)
DENSE_HALF = pltpu.VMEM((512, WIDE), BF16)
TILES = (8, TILE, TILE)


def cost(blocks):
    return pl.CostEstimate(
        flops=blocks * 2 * 256 * 1024 * 1024, bytes_accessed=blocks * 4 * 2**20, transcendentals=0
    )


def shards(tile_values, tile_coords, tile_counts, result_coords, result_counts):
    slot = jnp.arange(16, dtype=jnp.int32)
    at = jnp.pad(tile_coords[0, 0], (0, 12))
    code = jnp.where(slot < tile_counts[0, 0], at + (at >> 3), 8).astype(BF16)
    unit = jnp.concatenate(
        [tile_values.reshape(BODY, TILE), jnp.broadcast_to(code[:, None], (16, TILE))]
    )

    unit = lax.optimization_barrier(unit)

    def along(perm, v):
        return lax.ppermute(v, "loop", perm)

    def across(perm, v):
        return lax.ppermute(v, "group", perm)

    beside, crossed = along(YLO, unit), along(DIAGONAL, unit)
    pair = along(CORE, unit)
    first = jnp.concatenate([unit, pair])
    beside, crossed, _ = lax.optimization_barrier((beside, crossed, first))
    second = jnp.concatenate([beside, crossed])
    later, beside_later, _ = lax.optimization_barrier((unit, result_coords, first))
    row = jnp.concatenate([later, across(YHI, later)])
    at = jnp.pad(beside_later[0, 0], (0, 8))
    code = jnp.where(slot < result_counts[0, 0], at, at + 16).astype(BF16)
    codes = jnp.broadcast_to(code[:, None], (16, TILE))

    def after(v, *others):
        return lax.optimization_barrier((v, *others))

    streams = [first, second]
    right = [streams]
    row = jnp.concatenate([row, across(XNEAR, row)])
    left = [row, across(XMIRROR, row)]
    for r in range(3):
        ahead = along(RING, streams[0])
        behind = after(streams[1], ahead)[0] if r == 0 else streams[1]
        streams = [ahead, along(RING, behind)]
        other = after(*streams) if r < 2 else streams
        right += [streams, [along(CORE, v) for v in other]]
    last = [along(RING, v) for v in streams]

    limit = pltpu.CompilerParams(vmem_limit_bytes=24 * 2**20)
    dense_left, product = pl.pallas_call(
        begin,
        in_specs=[WHOLE] * 12,
        out_specs=[WHOLE] * 2,
        out_shape=[DENSE_LEFT, PRODUCT],
        scratch_shapes=[DENSE_RIGHT] * 2,
        compiler_params=limit,
        cost_estimate=cost(6),
    )(*sum(right[:5], []), *left)
    product = pl.pallas_call(
        add_half,
        in_specs=[WHOLE] * 3,
        out_specs=WHOLE,
        out_shape=PRODUCT,
        scratch_shapes=[DENSE_HALF],
        compiler_params=limit,
        cost_estimate=cost(1),
    )(last[0], dense_left, product)
    product = pl.pallas_call(
        proceed,
        in_specs=[WHOLE] * 6,
        out_specs=WHOLE,
        out_shape=PRODUCT,
        scratch_shapes=[DENSE_RIGHT] * 2,
        compiler_params=limit,
        cost_estimate=cost(2),
    )(*sum(right[5:], []), dense_left, product)
    squares, sums = pl.pallas_call(
        finish,
        in_specs=[WHOLE] * 4,
        out_specs=[AWAY, WHOLE],
        out_shape=[jax.ShapeDtypeStruct(TILES, F32), jax.ShapeDtypeStruct((32, 8, TILE), F32)],
        scratch_shapes=[
            DENSE_HALF,
            pltpu.VMEM((256, 1024), F32),
            pltpu.VMEM(TILES, F32),
            pltpu.SemaphoreType.DMA((8,)),
        ],
        compiler_params=limit,
        cost_estimate=cost(1),
    )(codes, last[1], dense_left, product)
    sums = lax.all_to_all(sums, "loop", 0, 0, tiled=True)
    out = pl.pallas_call(
        rescale,
        in_specs=[AWAY] * 3,
        out_specs=AWAY,
        out_shape=jax.ShapeDtypeStruct(TILES, F32),
        scratch_shapes=[
            pltpu.VMEM((16, TILE), BF16),
            pltpu.VMEM(TILES, F32),
            pltpu.VMEM((32, 8, TILE), F32),
            pltpu.VMEM(TILES, F32),
            pltpu.SemaphoreType.DMA((10,)),
            pltpu.SemaphoreType.DMA((8,)),
        ],
        compiler_params=limit,
    )(codes, squares, sums)
    return out[None, None]


def solution(mesh):
    placed = (
        P("loop", "group", None, None, None),
        P("loop", "group", None),
        P("loop", "group"),
        P("loop", "group", None),
        P("loop", "group"),
    )
    return jax.shard_map(
        shards,
        mesh=mesh,
        in_specs=placed,
        out_specs=P("loop", "group", None, None, None),
        check_vma=False,
    )
```

```python
import jax
import jax.numpy as jnp
from jax import lax
from jax.experimental import pallas as pl
from jax.experimental.pallas import tpu as pltpu
from jax.sharding import PartitionSpec as P

TILE = 128
SLOTS = 4
BODY = SLOTS * TILE
UNIT = BODY + 16
WIDE = 9 * TILE
F32, BF16 = jnp.float32, jnp.bfloat16


def loop_perm(f):
    pairs = []
    for i in range(32):
        z, y, c = f(i >> 2, (i >> 1) & 1, i & 1)
        pairs.append((i, (z % 8) * 4 + y * 2 + c))
    return pairs


def group_perm(f):
    pairs = []
    for i in range(8):
        x, y = f(i >> 1, i & 1)
        pairs.append((i, (x % 4) * 2 + y))
    return pairs


CORE = loop_perm(lambda z, y, c: (z, y, 1 - c))
YLO = loop_perm(lambda z, y, c: (z, 1 - y, c))
DIAGONAL = loop_perm(lambda z, y, c: (z, 1 - y, 1 - c))
RING = loop_perm(lambda z, y, c: (z + 1 - 2 * c, y, c))
YHI = group_perm(lambda x, y: (x, 1 - y))
XNEAR = group_perm(lambda x, y: (x ^ 1, y))
XMIRROR = group_perm(lambda x, y: (3 - x, y))


def scalars(ref, base, first, count):
    marks = ref[base : base + 16, :].astype(F32)
    return [jnp.max(marks[s : s + 1, :]).astype(jnp.int32) for s in range(first, first + count)]


def place(dst, ref, base, row):
    for s, code in enumerate(scalars(ref, base + BODY, 0, SLOTS)):
        r = (code >= 9).astype(jnp.int32)
        c = code - 9 * r
        rows = pl.ds(pl.multiple_of(row + r * TILE, TILE), TILE)
        cols = pl.ds(pl.multiple_of(c * TILE, TILE), TILE)
        dst[rows, cols] = ref[base + s * TILE : base + (s + 1) * TILE, :]


def where_am_i():
    i = lax.axis_index("loop")
    j = lax.axis_index("group")
    return i >> 2, (i >> 1) & 1, i & 1, j >> 1, j & 1


def multiply(dense_left, jobs, buffers):
    for k, (j, units) in enumerate(jobs):
        dense_right = buffers[k % len(buffers)]
        dense_right[...] = jnp.zeros_like(dense_right)
        for ref, base, y, c in units:
            place(dense_right, ref, base, (y * 2 + c) * 256)
        yield jnp.dot(
            dense_left[j, :, : 8 * TILE], dense_right[:, : 8 * TILE], preferred_element_type=F32
        )


def round_units(refs, y, c):
    pair, beside = refs
    return (
        (pair, 0, y, c),
        (pair, UNIT, y, 1 - c),
        (beside, 0, 1 - y, c),
        (beside, UNIT, 1 - y, 1 - c),
    )


def pack(values, coords, counts, unit, at, count, sem):
    copies = [
        pltpu.make_async_copy(coords, at, sem.at[0]),
        pltpu.make_async_copy(counts, count, sem.at[1]),
        pltpu.make_async_copy(values, unit.at[pl.ds(0, BODY)], sem.at[2]),
    ]
    for copy in copies:
        copy.start()
    copies[0].wait()
    copies[1].wait()
    row = lax.broadcasted_iota(jnp.int32, (16, TILE), 0)
    marks = jnp.full((16, TILE), 8, jnp.int32)
    for s in range(SLOTS):
        p = at[0, s]
        code = jnp.where(s < count[0, 0], p + (p >> 3), 8)
        marks = jnp.where(row == s, code, marks)
    unit[BODY:UNIT, :] = marks.astype(F32).astype(BF16)
    copies[2].wait()


def begin(*refs):
    own, rounds, left = refs[:2], refs[2:10], refs[10:12]
    dense_left, product, *dense_right = refs[12:]
    z, y, c, x, h = where_am_i()
    dense_left[...] = jnp.zeros_like(dense_left)
    for k in range(8):
        xx = (x, x ^ 1, 3 - x, (3 - x) ^ 1)[k >> 1]
        place(dense_left.at[xx * 2 + (h ^ (k & 1))], left[k >> 2], (k & 3) * UNIT, 0)
    sign = 1 - 2 * c
    jobs = [(z, round_units(own, y, c))]
    for r in (1, 2):
        near, far = rounds[4 * r - 4 : 4 * r - 2], rounds[4 * r - 2 : 4 * r]
        jobs.append(((z - sign * r) & 7, round_units(near, y, c)))
        jobs.append(((z + sign * r) & 7, round_units(far, y, 1 - c)))
    for k, part in enumerate(multiply(dense_left, jobs, dense_right)):
        product[...] = part if k == 0 else product[...] + part


def proceed(*refs):
    near, far = refs[:2], refs[2:4]
    dense_left, before, product, *dense_right = refs[4:]
    z, y, c, _, _ = where_am_i()
    sign = 1 - 2 * c
    jobs = [
        ((z - sign * 3) & 7, round_units(near, y, c)),
        ((z + sign * 3) & 7, round_units(far, y, 1 - c)),
    ]
    for k, part in enumerate(multiply(dense_left, jobs, dense_right)):
        product[...] = (before if k == 0 else product)[...] + part


def half(ref, y, c, dense_left, dense_half):
    z = where_am_i()[0]
    dense_half[...] = jnp.zeros_like(dense_half)
    place(dense_half, ref, 0, c * 256)
    place(dense_half, ref, UNIT, (1 - c) * 256)
    return jnp.dot(
        dense_left[(z + 4) & 7, :, pl.ds(pl.multiple_of(y * 512, 512), 512)],
        dense_half[:, : 8 * TILE],
        preferred_element_type=F32,
    )


def add_half(pair, dense_left, before, product, dense_half):
    _, y, c, _, _ = where_am_i()
    product[...] = before[...] + half(pair, y, c, dense_left, dense_half)


def finish(codes, beside, dense_left, before, squares, sums, dense_half, product, held, sem):
    _, y, c, _, _ = where_am_i()
    product[...] = before[...] + half(beside, 1 - y, c, dense_left, dense_half)
    column = lax.broadcasted_iota(jnp.int32, (8, TILE), 0)
    total = jnp.zeros((8, TILE), F32)
    copies = []
    for s, code in enumerate(scalars(codes, 0, 0, 8)):
        used = code < 16
        p = code & 15
        rows = pl.ds(pl.multiple_of((p >> 3) * TILE, TILE), TILE)
        cols = pl.ds(pl.multiple_of((p & 7) * TILE, TILE), TILE)
        tile = product[rows, cols]
        tile = jnp.where(used, tile * tile, 0.0)
        held[s] = tile
        copies.append(pltpu.make_async_copy(held.at[s], squares.at[s], sem.at[s]))
        copies[-1].start()
        part = jnp.sum(tile, axis=0, keepdims=True)
        total += jnp.where(column == (p & 7), part, 0.0)
    for k in range(32):
        sums[k] = total
    for copy in copies:
        copy.wait()


def rescale(codes, squares, sums, out, marks, inside, parts, done, sem_in, sem_out):
    ins = [pltpu.make_async_copy(sums, parts, sem_in.at[8])]
    ins.append(pltpu.make_async_copy(codes, marks, sem_in.at[9]))
    ins += [pltpu.make_async_copy(squares.at[s], inside.at[s], sem_in.at[s]) for s in range(8)]
    for copy in ins:
        copy.start()
    ins[1].wait()
    at = scalars(marks, 0, 0, 8)
    ins[0].wait()
    factor = 8192.0 / jnp.sum(parts[...], axis=0)
    column = lax.broadcasted_iota(jnp.int32, (8, TILE), 0)
    outs = []
    for s in range(8):
        pick = jnp.where(column == (at[s] & 7), factor, 0.0)
        pick = jnp.sum(pick, axis=0, keepdims=True)
        ins[2 + s].wait()
        done[s] = inside[s] * pick
        outs.append(pltpu.make_async_copy(done.at[s], out.at[s], sem_out.at[s]))
        outs[-1].start()
    for copy in outs:
        copy.wait()


WHOLE = pl.BlockSpec(memory_space=pltpu.VMEM)
AWAY = pl.BlockSpec(memory_space=pl.ANY)
DENSE_LEFT = jax.ShapeDtypeStruct((8, 256, WIDE), BF16)
PRODUCT = jax.ShapeDtypeStruct((256, 1024), F32)
DENSE_RIGHT = pltpu.VMEM((1024, WIDE), BF16)
DENSE_HALF = pltpu.VMEM((512, WIDE), BF16)
TILES = (8, TILE, TILE)


def cost(blocks):
    return pl.CostEstimate(
        flops=blocks * 2 * 256 * 1024 * 1024, bytes_accessed=blocks * 4 * 2**20, transcendentals=0
    )


def shards(tile_values, tile_coords, tile_counts, result_coords, result_counts):
    slot = jnp.arange(16, dtype=jnp.int32)
    unit = pl.pallas_call(
        pack,
        in_specs=[AWAY] * 3,
        out_specs=WHOLE,
        out_shape=jax.ShapeDtypeStruct((UNIT, TILE), BF16),
        scratch_shapes=[
            pltpu.SMEM((1, SLOTS), jnp.int32),
            pltpu.SMEM((1, 1), jnp.int32),
            pltpu.SemaphoreType.DMA((3,)),
        ],
        compiler_params=pltpu.CompilerParams(vmem_limit_bytes=60 * 2**20),
    )(tile_values.reshape(BODY, TILE), tile_coords.reshape(1, SLOTS), tile_counts)

    def along(perm, v):
        return lax.ppermute(v, "loop", perm)

    def across(perm, v):
        return lax.ppermute(v, "group", perm)

    beside, crossed = along(YLO, unit), along(DIAGONAL, unit)
    pair = along(CORE, unit)
    first = jnp.concatenate([unit, pair])
    beside, crossed, _ = lax.optimization_barrier((beside, crossed, first))
    second = jnp.concatenate([beside, crossed])
    later, beside_later, _ = lax.optimization_barrier((unit, result_coords, first))
    row = jnp.concatenate([later, across(YHI, later)])
    at = jnp.pad(beside_later[0, 0], (0, 8))
    code = jnp.where(slot < result_counts[0, 0], at, at + 16).astype(BF16)
    codes = jnp.broadcast_to(code[:, None], (16, TILE))

    def after(v, *others):
        return lax.optimization_barrier((v, *others))

    streams = [first, second]
    right = [streams]
    row = jnp.concatenate([row, across(XNEAR, row)])
    left = [row, across(XMIRROR, row)]
    for r in range(3):
        ahead = along(RING, streams[0])
        behind = after(streams[1], ahead)[0] if r == 0 else streams[1]
        streams = [ahead, along(RING, behind)]
        other = streams
        right += [streams, [along(CORE, v) for v in other]]
    last = [along(RING, v) for v in streams]

    limit = pltpu.CompilerParams(vmem_limit_bytes=24 * 2**20)
    dense_left, product = pl.pallas_call(
        begin,
        in_specs=[WHOLE] * 12,
        out_specs=[WHOLE] * 2,
        out_shape=[DENSE_LEFT, PRODUCT],
        scratch_shapes=[DENSE_RIGHT] * 2,
        compiler_params=limit,
        cost_estimate=cost(6),
    )(*sum(right[:5], []), *left)
    product = pl.pallas_call(
        add_half,
        in_specs=[WHOLE] * 3,
        out_specs=WHOLE,
        out_shape=PRODUCT,
        scratch_shapes=[DENSE_HALF],
        compiler_params=limit,
        cost_estimate=cost(1),
    )(last[0], dense_left, product)
    product = pl.pallas_call(
        proceed,
        in_specs=[WHOLE] * 6,
        out_specs=WHOLE,
        out_shape=PRODUCT,
        scratch_shapes=[DENSE_RIGHT] * 2,
        compiler_params=limit,
        cost_estimate=cost(2),
    )(*sum(right[5:], []), dense_left, product)
    squares, sums = pl.pallas_call(
        finish,
        in_specs=[WHOLE] * 4,
        out_specs=[AWAY, WHOLE],
        out_shape=[jax.ShapeDtypeStruct(TILES, F32), jax.ShapeDtypeStruct((32, 8, TILE), F32)],
        scratch_shapes=[
            DENSE_HALF,
            pltpu.VMEM((256, 1024), F32),
            pltpu.VMEM(TILES, F32),
            pltpu.SemaphoreType.DMA((8,)),
        ],
        compiler_params=limit,
        cost_estimate=cost(1),
    )(codes, last[1], dense_left, product)
    sums = lax.all_to_all(sums, "loop", 0, 0, tiled=True)
    out = pl.pallas_call(
        rescale,
        in_specs=[AWAY] * 3,
        out_specs=AWAY,
        out_shape=jax.ShapeDtypeStruct(TILES, F32),
        scratch_shapes=[
            pltpu.VMEM((16, TILE), BF16),
            pltpu.VMEM(TILES, F32),
            pltpu.VMEM((32, 8, TILE), F32),
            pltpu.VMEM(TILES, F32),
            pltpu.SemaphoreType.DMA((10,)),
            pltpu.SemaphoreType.DMA((8,)),
        ],
        compiler_params=limit,
    )(codes, squares, sums)
    return out[None, None]


def solution(mesh):
    placed = (
        P("loop", "group", None, None, None),
        P("loop", "group", None),
        P("loop", "group"),
        P("loop", "group", None),
        P("loop", "group"),
    )
    return jax.shard_map(
        shards,
        mesh=mesh,
        in_specs=placed,
        out_specs=P("loop", "group", None, None, None),
        check_vma=False,
    )
```
